128 devices in a mesh: wide: 64 (over z, x, y_hi, core), narrow: 2 (over y_lo).
Axes of the slice: x: 4, y: 4 (y_hi: 2, y_lo: 2; y = y_hi * 2 + y_lo), z: 4, core: 2. Of those that a mesh axis runs over, the one named last changes fastest.
Arguments:
- coeffs: float32 [7680, 7680], P('narrow', 'wide'), may hold values from -6 to 6
- diagonal: float32 [7680, 7680], P('narrow', 'wide'), may hold values from 0.5 to 3
- tile_cols: int32 [60, 20], P('narrow'), may hold values from 0 to 59, as said below
- tile_vals: bfloat16 [60, 20, 128, 128], P('narrow'), may hold values from -3 to 3, as said below
Outputs:
- sigma: float32 [7680, 7680], P('narrow', 'wide')
The draws below stay inside these ranges and needn't reach their ends.
Inputs may be any that keep to these rules, and one draw needn't show every extreme that they name: `tile_cols`: row I lists 20 different tile columns, never I itself; J is listed in row I exactly when I is listed in row J. Where tile_cols[I, k] = J and tile_cols[J, m] = I, tile_vals[J, m] is the transpose of tile_vals[I, k], so H is symmetric.
All inputs are finite; a program needn't handle non-finite values.
Results may differ from the reference program's by a relative error of at most 0.0023.
Values may be sent and summed in bfloat16 or wider, within the bound.
A program may use at most 192 MiB of HBM per device.

```python
import math
import jax
import jax.numpy as jnp
from jax import lax

TILE = 128
DEG = 20
NT = 60
STRINGS = 7680


def pattern(key):
    key_order, key_offset = jax.random.split(key)
    shuffle = jax.random.permutation(key_order, NT).astype(jnp.int32)
    offsets = jax.random.permutation(key_offset, NT // 2 - 1)[:DEG // 2].astype(jnp.int32) + 1
    return (shuffle, offsets)


def draw_tile_cols(key, part):
    shuffle, offsets = pattern(key)
    inverse = jnp.zeros((NT,), jnp.int32).at[shuffle].set(jnp.arange(NT, dtype=jnp.int32))
    both_steps = jnp.concatenate([offsets, NT - offsets])
    places = (shuffle[:, None] + both_steps[None, :]) % NT
    return inverse[places].astype(jnp.int32)


def draw_tile_vals(key, part):
    shuffle, offsets = pattern(key)
    key = jax.random.fold_in(key, 7)
    half_count = DEG // 2
    drawn = jax.random.truncated_normal(key, -3.0, 3.0, (NT, half_count, TILE, TILE), jnp.float32)
    forward = drawn[shuffle]
    back_pos = (shuffle[:, None] - offsets[None, :]) % NT
    backward = drawn[back_pos, jnp.arange(half_count, dtype=jnp.int32)[None, :]]
    backward = jnp.swapaxes(backward, -1, -2)
    return jnp.concatenate([forward, backward], axis=1).astype(jnp.bfloat16)


def levels(stream_key, extent, pieces, smallest, high):
    def one(position, shards_of):
        draws = jax.random.uniform(jax.random.fold_in(jax.random.fold_in(stream_key, 6), position), (shards_of,), jnp.float32, smallest / len(pieces), high / len(pieces))
        return jnp.repeat(jnp.exp(draws), extent[position] // shards_of).reshape((-1,) + (1,) * (len(extent) - position - 1))

    gain = one(*pieces[0])
    for cut in pieces[1:]:
        gain = gain * one(*cut)
    return gain


def bell_draw(key, shape, width, reach, cuts=(), kind=jnp.bfloat16):
    array = jax.random.normal(key, shape, jnp.float32) * width
    if len(cuts) > 0:
        array = levels(key, shape, cuts, -0.22, 0.18) * array
    return jnp.clip(array, min=-reach, max=reach).astype(kind)


def setup_inputs(seed: int = 0) -> dict:
    streams_of = jax.random.split(jax.random.key(seed), 5)
    return {
        "coeffs": bell_draw(streams_of[0], (STRINGS, STRINGS), 1.0, 6.0, ((0, 2), (1, 64)), jnp.float32),
        "diagonal": jnp.clip(0.5 + 2.5 * jax.random.uniform(streams_of[1], (STRINGS, STRINGS), jnp.float32) ** levels(streams_of[1], (STRINGS, STRINGS), ((0, 2), (1, 64)), -0.2, 0.2), 0.5, 3.0),
        "tile_cols": draw_tile_cols(jax.random.fold_in(streams_of[4], 71), 0),
        "tile_vals": draw_tile_vals(jax.random.fold_in(streams_of[4], 71), 0),
    }


def reference(coeffs, diagonal, tile_cols, tile_vals):
    weight_scale = 1.0 / math.sqrt(DEG * TILE)
    coeff_low = coeffs.astype(jnp.bfloat16)
    row_blocks = coeff_low.reshape(NT, TILE, NT * TILE)
    col_blocks = coeff_low.reshape(NT * TILE, NT, TILE)

    def alpha_row(row_index):
        picked = row_blocks[tile_cols[row_index]].astype(jnp.float32)
        return jnp.einsum('kab,kbm->am', tile_vals[row_index].astype(jnp.float32), picked)

    def beta_row(row_index):
        picked = col_blocks[:, tile_cols[row_index]].astype(jnp.float32)
        return jnp.einsum('akb,kcb->ac', picked, tile_vals[row_index].astype(jnp.float32))
    rows_all = jnp.arange(NT, dtype=jnp.int32)
    sigma_alpha = lax.map(alpha_row, rows_all).reshape(NT * TILE, NT * TILE)
    sigma_beta = lax.map(beta_row, rows_all)
    sigma_beta = jnp.transpose(sigma_beta, (1, 0, 2)).reshape(NT * TILE, NT * TILE)
    return weight_scale * sigma_alpha + weight_scale * sigma_beta + diagonal * coeffs
```

```python
import functools
import math

import jax
import jax.numpy as jnp
from jax import lax
from jax.experimental import pallas as pl
from jax.experimental.pallas import tpu as pltpu
from jax.sharding import PartitionSpec as P

MESH = pl.DeviceIdType.MESH
TILE = 128
PER_PLANE = 16
TILES_PER_PLANE = 15


def kernel(
    cols_ref,
    coeff_hbm,
    diag_hbm,
    vals_hbm,
    out_ref,
    coeff_v,
    diag_v,
    vals_v,
    x_ref,
    y_ref,
    yt_ref,
    acc_ref,
    alpha_ref,
    send_ref,
    back_ref,
    local_sem,
    pair_send,
    pair_recv,
    fwd_send,
    fwd_recv,
    ret_send,
    ret_recv,
    *,
    wide,
    scale,
):
    w = lax.axis_index("wide")
    n = lax.axis_index("narrow")
    other = 1 - n
    half = out_ref.shape[1] // TILE
    width = out_ref.shape[0]
    degree = cols_ref.shape[1]
    half_wide = wide // 2

    coeff_copy = pltpu.make_async_copy(coeff_hbm, coeff_v, local_sem.at[0])
    coeff_copy.start()
    vals_copy = pltpu.make_async_copy(vals_hbm, vals_v, local_sem.at[1])
    vals_copy.start()
    diag_copy = pltpu.make_async_copy(diag_hbm, diag_v, local_sem.at[2])
    diag_copy.start()
    coeff_copy.wait()

    for i in range(half):
        x_ref[n * half + i] = coeff_v[:, i * TILE : (i + 1) * TILE].astype(jnp.bfloat16)

    own_half = x_ref.at[pl.ds(n * half, half)]
    pair = pltpu.make_async_remote_copy(
        src_ref=own_half,
        dst_ref=own_half,
        send_sem=pair_send,
        recv_sem=pair_recv,
        device_id=(w, other),
        device_id_type=MESH,
    )
    pair.start()

    def send_forward(step, carry):
        i = lax.rem(w + step, half)
        tile = n * half + i
        to = tile + tile // TILES_PER_PLANE
        for to_n in (0, 1):
            mine = jnp.logical_and(to == w, n == to_n)

            @pl.when(mine)
            def _():
                pltpu.make_async_copy(x_ref.at[tile], y_ref.at[w], fwd_recv).start()

            @pl.when(jnp.logical_not(mine))
            def _():
                pltpu.make_async_remote_copy(
                    src_ref=x_ref.at[tile],
                    dst_ref=y_ref.at[w],
                    send_sem=fwd_send,
                    recv_sem=fwd_recv,
                    device_id=(to, to_n),
                    device_id_type=MESH,
                ).start()

        return carry

    lax.fori_loop(0, half, send_forward, 0)

    group = w // PER_PLANE
    place = lax.rem(w, PER_PLANE)
    active = place < TILES_PER_PLANE
    my_tile = group * TILES_PER_PLANE + place
    tile_half = my_tile // half
    slot = lax.rem(my_tile, half)

    vals_copy.wait()
    pair.wait_recv()

    def alpha_step(row, carry):
        lhs = jnp.concatenate([x_ref[cols_ref[row, k]] for k in range(degree)], axis=1)
        rhs = jnp.concatenate([vals_v[row, k] for k in range(degree)], axis=1)
        alpha_ref[row] = lax.dot_general(
            lhs, rhs, (((1,), (1,)), ((), ())), preferred_element_type=jnp.float32
        )
        return carry

    lax.fori_loop(0, half, alpha_step, 0)

    @pl.when(active)
    def _():
        pltpu.make_async_copy(y_ref, y_ref, fwd_recv).wait()

        def repack(g, carry):
            for t in range(TILES_PER_PLANE):
                low, high = t * TILE, (t + 1) * TILE
                pieces = []
                while low < high:
                    source, begin = low // width, low % width
                    end = min(width, begin + high - low)
                    piece = y_ref[g * PER_PLANE + source].astype(jnp.float32)
                    pieces.append(piece[begin:end])
                    low += end - begin
                yt_ref[g * TILES_PER_PLANE + t] = jnp.concatenate(pieces, axis=0).astype(
                    jnp.bfloat16
                )
            return carry

        lax.fori_loop(0, wide // PER_PLANE, repack, 0)

        def send_chunk(j):
            send_ref[j] = acc_ref[pl.ds(pl.multiple_of(j * width, 8), width), :].astype(
                jnp.bfloat16
            )
            to = n * half_wide + j
            mine = jnp.logical_and(to == w, tile_half == n)

            @pl.when(mine)
            def _():
                pltpu.make_async_copy(send_ref.at[j], back_ref.at[slot], ret_recv).start()

            @pl.when(jnp.logical_not(mine))
            def _():
                pltpu.make_async_remote_copy(
                    src_ref=send_ref.at[j],
                    dst_ref=back_ref.at[slot],
                    send_sem=ret_send,
                    recv_sem=ret_recv,
                    device_id=(to, tile_half),
                    device_id_type=MESH,
                ).start()

        def chunk_of(row):
            return row + row // TILES_PER_PLANE

        first = lax.rem(w * 7, half)

        def beta_step(step, carry):
            row = lax.rem(first + step, half)
            lhs = jnp.concatenate([vals_v[row, k] for k in range(degree)], axis=1)
            rhs = jnp.concatenate(
                [yt_ref[cols_ref[row, k]] for k in range(degree)],
                axis=0,
            )
            acc_ref[pl.ds(pl.multiple_of(row * TILE, TILE), TILE), :] = jnp.dot(
                lhs, rhs, preferred_element_type=jnp.float32
            )

            @pl.when(step > 0)
            def _():
                send_chunk(chunk_of(row))

            @pl.when(lax.rem(row, TILES_PER_PLANE) == TILES_PER_PLANE - 1)
            def _():
                send_chunk(chunk_of(row) + 1)

            return carry

        lax.fori_loop(0, half, beta_step, 0)
        send_chunk(chunk_of(first))

    diag_copy.wait()
    pltpu.make_async_copy(back_ref, back_ref, ret_recv).wait()

    for i in range(half):
        part = slice(i * TILE, (i + 1) * TILE)
        out_ref[:, part] = (
            scale * alpha_ref[i]
            + scale * back_ref[i].astype(jnp.float32)
            + diag_v[:, part] * coeff_v[:, part]
        )

    pair.wait_send()
    has_own = jnp.logical_and(active, tile_half == n)

    @pl.when(has_own)
    def _():
        pltpu.make_async_copy(
            x_ref.at[pl.ds(0, 2 * half - 1)], x_ref.at[pl.ds(0, 2 * half - 1)], fwd_send
        ).wait()

    @pl.when(jnp.logical_not(has_own))
    def _():
        pltpu.make_async_copy(x_ref, x_ref, fwd_send).wait()

    own_return = jnp.logical_and(has_own, w // half_wide == n)

    @pl.when(jnp.logical_and(active, own_return))
    def _():
        done = send_ref.at[pl.ds(0, half_wide - 1)]
        pltpu.make_async_copy(done, done, ret_send).wait()

    @pl.when(jnp.logical_and(active, jnp.logical_not(own_return)))
    def _():
        pltpu.make_async_copy(send_ref, send_ref, ret_send).wait()


def solution(mesh):
    wide = mesh.shape["wide"]

    def per_device(coeffs, diagonal, tile_cols, tile_vals):
        rows, width = coeffs.shape
        half, degree = tile_cols.shape
        scale = 1.0 / math.sqrt(degree * TILE)
        any_space = pl.BlockSpec(memory_space=pl.ANY)
        out = pl.pallas_call(
            functools.partial(kernel, wide=wide, scale=scale),
            out_shape=jax.ShapeDtypeStruct((width, rows), jnp.float32),
            in_specs=[
                pl.BlockSpec(memory_space=pltpu.SMEM),
                any_space,
                any_space,
                any_space,
            ],
            out_specs=pl.BlockSpec(memory_space=pltpu.VMEM),
            scratch_shapes=[
                pltpu.VMEM((width, rows), jnp.float32),
                pltpu.VMEM((width, rows), jnp.float32),
                pltpu.VMEM((half, degree, TILE, TILE), jnp.bfloat16),
                pltpu.VMEM((2 * half, width, TILE), jnp.bfloat16),
                pltpu.VMEM((wide, width, TILE), jnp.bfloat16),
                pltpu.VMEM((2 * half, TILE, TILE), jnp.bfloat16),
                pltpu.VMEM((rows, TILE), jnp.float32),
                pltpu.VMEM((half, width, TILE), jnp.float32),
                pltpu.VMEM((wide // 2, width, TILE), jnp.bfloat16),
                pltpu.VMEM((half, width, TILE), jnp.bfloat16),
                pltpu.SemaphoreType.DMA((3,)),
                pltpu.SemaphoreType.DMA,
                pltpu.SemaphoreType.DMA,
                pltpu.SemaphoreType.DMA,
                pltpu.SemaphoreType.DMA,
                pltpu.SemaphoreType.DMA,
                pltpu.SemaphoreType.DMA,
            ],
            compiler_params=pltpu.CompilerParams(
                has_side_effects=True, vmem_limit_bytes=52 * 1024 * 1024
            ),
        )(tile_cols, coeffs.T, diagonal.T, tile_vals)
        return out.T

    in_specs = (
        P("narrow", "wide"),
        P("narrow", "wide"),
        P("narrow", None),
        P("narrow", None, None, None),
    )
    return jax.shard_map(
        per_device,
        mesh=mesh,
        in_specs=in_specs,
        out_specs=P("narrow", "wide"),
        check_vma=False,
    )
```

```python
import functools
import math

import jax
import jax.numpy as jnp
from jax import lax
from jax.experimental import pallas as pl
from jax.experimental.pallas import tpu as pltpu
from jax.sharding import PartitionSpec as P

MESH = pl.DeviceIdType.MESH
TILE = 128
PIECES = 5
PER_SIDE = 16
GROUP_SLICES = 16
GROUP_TILES = 15


def kernel(
    cols_ref,
    coeff_hbm,
    diag_hbm,
    vals_hbm,
    out_ref,
    coeff_v,
    diag_v,
    vals_v,
    x_ref,
    y_ref,
    yt_ref,
    acc_ref,
    alpha_ref,
    send_ref,
    back_ref,
    local_sem,
    pair_send,
    pair_recv,
    fwd_send,
    fwd_recv,
    ret_send,
    ret_recv,
    *,
    wide,
    scale,
):
    w = lax.axis_index("wide")
    n = lax.axis_index("narrow")
    other = 1 - n
    half = out_ref.shape[1] // TILE
    width = out_ref.shape[0]
    degree = cols_ref.shape[0]
    half_wide = wide // 2

    coeff_copy = pltpu.make_async_copy(coeff_hbm, coeff_v, local_sem.at[0])
    coeff_copy.start()
    vals_copy = pltpu.make_async_copy(vals_hbm, vals_v, local_sem.at[1])
    vals_copy.start()
    diag_copy = pltpu.make_async_copy(diag_hbm, diag_v, local_sem.at[2])
    diag_copy.start()

    barrier = pltpu.get_barrier_semaphore()

    def greet(step, carry):
        to = lax.rem(w + step, wide)

        @pl.when(step > 0)
        def _():
            pl.semaphore_signal(barrier, inc=1, device_id=(to, n), device_id_type=MESH)

        pl.semaphore_signal(barrier, inc=1, device_id=(to, other), device_id_type=MESH)
        return carry

    lax.fori_loop(0, wide, greet, 0)
    coeff_copy.wait()

    for i in range(half):
        x_ref[n * half + i] = coeff_v[:, i * TILE : (i + 1) * TILE].astype(jnp.bfloat16)

    pl.semaphore_wait(barrier, 2 * wide - 1)

    piece = half // PIECES
    pair = []
    for j in range(PIECES):
        part = x_ref.at[pl.ds(n * half + j * piece, piece)]
        copy = pltpu.make_async_remote_copy(
            src_ref=part,
            dst_ref=part,
            send_sem=pair_send.at[j],
            recv_sem=pair_recv.at[j],
            device_id=(w, other),
            device_id_type=MESH,
        )
        copy.start()
        pair.append(copy)

    my_plane = lax.rem(w // 2, 2)

    def send_forward(tile):
        side, rank = tile // half, lax.rem(tile, half)
        plane = lax.rem(rank, 2)
        spot = side * (PER_SIDE - 1) + rank // 2
        spot = spot + spot // (PER_SIDE - 1)
        to = (spot // 2) * 4 + plane * 2 + lax.rem(spot, 2)
        to_n = jnp.where(plane == my_plane, n, other)
        mine = jnp.logical_and(to == w, to_n == n)

        @pl.when(mine)
        def _():
            pltpu.make_async_copy(x_ref.at[tile], y_ref.at[w], fwd_recv).start()

        @pl.when(jnp.logical_not(mine))
        def _():
            pltpu.make_async_remote_copy(
                src_ref=x_ref.at[tile],
                dst_ref=y_ref.at[w],
                send_sem=fwd_send,
                recv_sem=fwd_recv,
                device_id=(to, to_n),
                device_id_type=MESH,
            ).start()

    def send_own(step, carry):
        send_forward(n * half + lax.rem(w * 7 + step, half))
        return carry

    lax.fori_loop(0, half, send_own, 0)

    for j in range(PIECES):
        pair[j].wait_recv()

        def send_relayed(step, carry):
            send_forward(other * half + j * piece + lax.rem(w + step, piece))
            return carry

        lax.fori_loop(0, piece, send_relayed, 0)

    my_spot = (w // 4) * 2 + lax.rem(w, 2)
    tile_half = my_spot // PER_SIDE
    place = lax.rem(my_spot, PER_SIDE)
    active = place < PER_SIDE - 1
    slot = place * 2 + my_plane

    vals_copy.wait()

    @pl.when(active)
    def _():
        pltpu.make_async_copy(y_ref, y_ref, fwd_recv).wait()

        def repack(g, carry):
            for t in range(GROUP_TILES):
                low, high = t * TILE, (t + 1) * TILE
                pieces = []
                while low < high:
                    source, begin = low // width, low % width
                    end = min(width, begin + high - low)
                    piece = y_ref[g * GROUP_SLICES + source].astype(jnp.float32)
                    pieces.append(piece[begin:end])
                    low += end - begin
                yt_ref[g * GROUP_TILES + t] = jnp.concatenate(pieces, axis=0).astype(
                    jnp.bfloat16
                )
            return carry

        lax.fori_loop(0, wide // GROUP_SLICES, repack, 0)

        def send_chunk(j):
            send_ref[j] = acc_ref[pl.ds(pl.multiple_of(j * width, 8), width), :].astype(
                jnp.bfloat16
            )
            to = n * half_wide + j
            mine = jnp.logical_and(to == w, tile_half == n)

            @pl.when(mine)
            def _():
                pltpu.make_async_copy(send_ref.at[j], back_ref.at[slot], ret_recv).start()

            @pl.when(jnp.logical_not(mine))
            def _():
                pltpu.make_async_remote_copy(
                    src_ref=send_ref.at[j],
                    dst_ref=back_ref.at[slot],
                    send_sem=ret_send,
                    recv_sem=ret_recv,
                    device_id=(to, tile_half),
                    device_id_type=MESH,
                ).start()

        def chunk_of(row):
            return row + row // GROUP_TILES

        first = lax.rem(w * 7, half)

        def beta_step(step, carry):
            row = lax.rem(first + step, half)
            lhs = jnp.concatenate([vals_v[row, k] for k in range(degree)], axis=1)
            rhs = jnp.concatenate(
                [yt_ref[cols_ref[k, row]] for k in range(degree)],
                axis=0,
            )
            acc_ref[pl.ds(pl.multiple_of(row * TILE, TILE), TILE), :] = jnp.dot(
                lhs, rhs, preferred_element_type=jnp.float32
            )

            @pl.when(step > 0)
            def _():
                send_chunk(chunk_of(row))

            @pl.when(lax.rem(row, GROUP_TILES) == GROUP_TILES - 1)
            def _():
                send_chunk(chunk_of(row) + 1)

            return carry

        lax.fori_loop(0, half, beta_step, 0)
        send_chunk(chunk_of(first))

    def alpha_step(row, carry):
        lhs = jnp.concatenate([x_ref[cols_ref[k, row]] for k in range(degree)], axis=1)
        rhs = jnp.concatenate([vals_v[row, k] for k in range(degree)], axis=1)
        alpha_ref[row] = lax.dot_general(
            lhs, rhs, (((1,), (1,)), ((), ())), preferred_element_type=jnp.float32
        )
        return carry

    lax.fori_loop(0, half, alpha_step, 0)

    diag_copy.wait()
    pltpu.make_async_copy(back_ref, back_ref, ret_recv).wait()

    for i in range(half):
        part = slice(i * TILE, (i + 1) * TILE)
        out_ref[:, part] = (
            scale * alpha_ref[i]
            + scale * back_ref[i].astype(jnp.float32)
            + diag_v[:, part] * coeff_v[:, part]
        )

    for copy in pair:
        copy.wait_send()

    @pl.when(active)
    def _():
        done = x_ref.at[pl.ds(0, 2 * half - 1)]
        pltpu.make_async_copy(done, done, fwd_send).wait()

    @pl.when(jnp.logical_not(active))
    def _():
        pltpu.make_async_copy(x_ref, x_ref, fwd_send).wait()

    own_return = jnp.logical_and(tile_half == n, w // half_wide == n)

    @pl.when(jnp.logical_and(active, own_return))
    def _():
        done = send_ref.at[pl.ds(0, half_wide - 1)]
        pltpu.make_async_copy(done, done, ret_send).wait()

    @pl.when(jnp.logical_and(active, jnp.logical_not(own_return)))
    def _():
        pltpu.make_async_copy(send_ref, send_ref, ret_send).wait()


def solution(mesh):
    wide = mesh.shape["wide"]

    def per_device(coeffs, diagonal, tile_cols, tile_vals):
        rows, width = coeffs.shape
        half, degree = tile_cols.shape
        scale = 1.0 / math.sqrt(degree * TILE)
        any_space = pl.BlockSpec(memory_space=pl.ANY)
        out = pl.pallas_call(
            functools.partial(kernel, wide=wide, scale=scale),
            out_shape=jax.ShapeDtypeStruct((width, rows), jnp.float32),
            in_specs=[
                pl.BlockSpec(memory_space=pltpu.SMEM),
                any_space,
                any_space,
                any_space,
            ],
            out_specs=pl.BlockSpec(memory_space=pltpu.VMEM),
            scratch_shapes=[
                pltpu.VMEM((width, rows), jnp.float32),
                pltpu.VMEM((width, rows), jnp.float32),
                pltpu.VMEM((half, degree, TILE, TILE), jnp.bfloat16),
                pltpu.VMEM((2 * half, width, TILE), jnp.bfloat16),
                pltpu.VMEM((wide, width, TILE), jnp.bfloat16),
                pltpu.VMEM((2 * half, TILE, TILE), jnp.bfloat16),
                pltpu.VMEM((rows, TILE), jnp.float32),
                pltpu.VMEM((half, width, TILE), jnp.float32),
                pltpu.VMEM((wide // 2, width, TILE), jnp.bfloat16),
                pltpu.VMEM((half, width, TILE), jnp.bfloat16),
                pltpu.SemaphoreType.DMA((3,)),
                pltpu.SemaphoreType.DMA((PIECES,)),
                pltpu.SemaphoreType.DMA((PIECES,)),
                pltpu.SemaphoreType.DMA,
                pltpu.SemaphoreType.DMA,
                pltpu.SemaphoreType.DMA,
                pltpu.SemaphoreType.DMA,
            ],
            compiler_params=pltpu.CompilerParams(
                collective_id=0, has_side_effects=True, vmem_limit_bytes=52 * 1024 * 1024
            ),
        )(tile_cols.T, coeffs.T, diagonal.T, tile_vals)
        return out.T

    in_specs = (
        P("narrow", "wide"),
        P("narrow", "wide"),
        P("narrow", None),
        P("narrow", None, None, None),
    )
    return jax.shard_map(
        per_device,
        mesh=mesh,
        in_specs=in_specs,
        out_specs=P("narrow", "wide"),
        check_vma=False,
    )
```

```python
import functools
import math

import jax
import jax.numpy as jnp
from jax import lax
from jax.experimental import pallas as pl
from jax.experimental.pallas import tpu as pltpu
from jax.sharding import PartitionSpec as P

MESH = pl.DeviceIdType.MESH
TILE = 128
PIECES = (9, 8, 6, 4, 2, 1)
GROUP_SLICES = 16
GROUP_TILES = 15


def kernel(
    cols_ref,
    coeff_hbm,
    diag_hbm,
    vals_hbm,
    out_ref,
    coeff_v,
    diag_v,
    vals_v,
    x_ref,
    y_ref,
    yt_ref,
    acc_ref,
    alpha_ref,
    send_ref,
    back_ref,
    local_sem,
    pair_send,
    pair_recv,
    fwd_send,
    fwd_recv,
    ret_send,
    ret_recv,
    *,
    wide,
    scale,
):
    w = lax.axis_index("wide")
    n = lax.axis_index("narrow")
    other = 1 - n
    half = out_ref.shape[1] // TILE
    width = out_ref.shape[0]
    degree = cols_ref.shape[0]
    half_wide = wide // 2

    coeff_copy = pltpu.make_async_copy(coeff_hbm, coeff_v, local_sem.at[0])
    coeff_copy.start()
    vals_copy = pltpu.make_async_copy(vals_hbm, vals_v, local_sem.at[1])
    vals_copy.start()
    diag_copy = pltpu.make_async_copy(diag_hbm, diag_v, local_sem.at[2])
    diag_copy.start()

    barrier = pltpu.get_barrier_semaphore()

    def greet(step, carry):
        to = lax.rem(w + step, wide)

        @pl.when(step > 0)
        def _():
            pl.semaphore_signal(barrier, inc=1, device_id=(to, n), device_id_type=MESH)

        pl.semaphore_signal(barrier, inc=1, device_id=(to, other), device_id_type=MESH)
        return carry

    lax.fori_loop(0, wide, greet, 0)
    coeff_copy.wait()

    for i in range(half):
        x_ref[n * half + i] = coeff_v[:, i * TILE : (i + 1) * TILE].astype(jnp.bfloat16)

    pl.semaphore_wait(barrier, 2 * wide - 1)

    starts = [sum(PIECES[:j]) for j in range(len(PIECES))]
    pair = []
    for j, piece in enumerate(PIECES):
        part = x_ref.at[pl.ds(n * half + starts[j], piece)]
        copy = pltpu.make_async_remote_copy(
            src_ref=part,
            dst_ref=part,
            send_sem=pair_send.at[j],
            recv_sem=pair_recv.at[j],
            device_id=(w, other),
            device_id_type=MESH,
        )
        copy.start()
        pair.append(copy)

    my_plane = lax.rem(w // 2, 2)

    def send_forward(tile):
        side, rank = tile // half, lax.rem(tile, half)
        plane = lax.rem(rank, 2)
        to = (rank // 2) * 4 + plane * 2 + side
        to_n = jnp.where(plane == my_plane, n, other)
        mine = jnp.logical_and(to == w, to_n == n)

        @pl.when(mine)
        def _():
            pltpu.make_async_copy(x_ref.at[tile], y_ref.at[w], fwd_recv).start()

        @pl.when(jnp.logical_not(mine))
        def _():
            pltpu.make_async_remote_copy(
                src_ref=x_ref.at[tile],
                dst_ref=y_ref.at[w],
                send_sem=fwd_send,
                recv_sem=fwd_recv,
                device_id=(to, to_n),
                device_id_type=MESH,
            ).start()

    def send_own(step, carry):
        send_forward(n * half + lax.rem(w * 7 + step, half))
        return carry

    lax.fori_loop(0, half, send_own, 0)

    for j, piece in enumerate(PIECES):
        pair[j].wait_recv()

        def send_relayed(step, carry):
            send_forward(other * half + starts[j] + lax.rem(w + step, piece))
            return carry

        lax.fori_loop(0, piece, send_relayed, 0)

    tile_half = lax.rem(w, 2)
    place = w // 4
    active = place < half // 2
    slot = place * 2 + my_plane

    vals_copy.wait()

    def alpha_step(row, carry):
        lhs = jnp.concatenate([x_ref[cols_ref[k, row]] for k in range(degree)], axis=1)
        rhs = jnp.concatenate([vals_v[row, k] for k in range(degree)], axis=1)
        alpha_ref[row] = lax.dot_general(
            lhs, rhs, (((1,), (1,)), ((), ())), preferred_element_type=jnp.float32
        )
        return carry

    lax.fori_loop(0, half, alpha_step, 0)

    @pl.when(active)
    def _():
        pltpu.make_async_copy(y_ref, y_ref, fwd_recv).wait()

        def repack(g, carry):
            for t in range(GROUP_TILES):
                low, high = t * TILE, (t + 1) * TILE
                pieces = []
                while low < high:
                    source, begin = low // width, low % width
                    end = min(width, begin + high - low)
                    piece = y_ref[g * GROUP_SLICES + source].astype(jnp.float32)
                    pieces.append(piece[begin:end])
                    low += end - begin
                yt_ref[g * GROUP_TILES + t] = jnp.concatenate(pieces, axis=0).astype(
                    jnp.bfloat16
                )
            return carry

        lax.fori_loop(0, wide // GROUP_SLICES, repack, 0)

        def send_chunk(j):
            send_ref[j] = acc_ref[pl.ds(pl.multiple_of(j * width, 8), width), :].astype(
                jnp.bfloat16
            )
            to = n * half_wide + j
            mine = jnp.logical_and(to == w, tile_half == n)

            @pl.when(mine)
            def _():
                pltpu.make_async_copy(send_ref.at[j], back_ref.at[slot], ret_recv).start()

            @pl.when(jnp.logical_not(mine))
            def _():
                pltpu.make_async_remote_copy(
                    src_ref=send_ref.at[j],
                    dst_ref=back_ref.at[slot],
                    send_sem=ret_send,
                    recv_sem=ret_recv,
                    device_id=(to, tile_half),
                    device_id_type=MESH,
                ).start()

        def chunk_of(row):
            return row + row // GROUP_TILES

        first = lax.rem(w * 7, half)

        def beta_step(step, carry):
            row = lax.rem(first + step, half)
            lhs = jnp.concatenate([vals_v[row, k] for k in range(degree)], axis=1)
            rhs = jnp.concatenate(
                [yt_ref[cols_ref[k, row]] for k in range(degree)],
                axis=0,
            )
            acc_ref[pl.ds(pl.multiple_of(row * TILE, TILE), TILE), :] = jnp.dot(
                lhs, rhs, preferred_element_type=jnp.float32
            )

            @pl.when(step > 0)
            def _():
                send_chunk(chunk_of(row))

            @pl.when(lax.rem(row, GROUP_TILES) == GROUP_TILES - 1)
            def _():
                send_chunk(chunk_of(row) + 1)

            return carry

        lax.fori_loop(0, half, beta_step, 0)
        send_chunk(chunk_of(first))

    diag_copy.wait()
    pltpu.make_async_copy(back_ref, back_ref, ret_recv).wait()

    for i in range(half):
        part = slice(i * TILE, (i + 1) * TILE)
        out_ref[:, part] = (
            scale * alpha_ref[i]
            + scale * back_ref[i].astype(jnp.float32)
            + diag_v[:, part] * coeff_v[:, part]
        )

    for copy in pair:
        copy.wait_send()

    @pl.when(active)
    def _():
        done = x_ref.at[pl.ds(0, 2 * half - 1)]
        pltpu.make_async_copy(done, done, fwd_send).wait()

    @pl.when(jnp.logical_not(active))
    def _():
        pltpu.make_async_copy(x_ref, x_ref, fwd_send).wait()

    own_return = jnp.logical_and(tile_half == n, w // half_wide == n)

    @pl.when(jnp.logical_and(active, own_return))
    def _():
        done = send_ref.at[pl.ds(0, half_wide - 1)]
        pltpu.make_async_copy(done, done, ret_send).wait()

    @pl.when(jnp.logical_and(active, jnp.logical_not(own_return)))
    def _():
        pltpu.make_async_copy(send_ref, send_ref, ret_send).wait()


def solution(mesh):
    wide = mesh.shape["wide"]

    def per_device(coeffs, diagonal, tile_cols, tile_vals):
        rows, width = coeffs.shape
        half, degree = tile_cols.shape
        scale = 1.0 / math.sqrt(degree * TILE)
        any_space = pl.BlockSpec(memory_space=pl.ANY)
        out = pl.pallas_call(
            functools.partial(kernel, wide=wide, scale=scale),
            out_shape=jax.ShapeDtypeStruct((width, rows), jnp.float32),
            in_specs=[
                pl.BlockSpec(memory_space=pltpu.SMEM),
                any_space,
                any_space,
                any_space,
            ],
            out_specs=pl.BlockSpec(memory_space=pltpu.VMEM),
            scratch_shapes=[
                pltpu.VMEM((width, rows), jnp.float32),
                pltpu.VMEM((width, rows), jnp.float32),
                pltpu.VMEM((half, degree, TILE, TILE), jnp.bfloat16),
                pltpu.VMEM((2 * half, width, TILE), jnp.bfloat16),
                pltpu.VMEM((wide, width, TILE), jnp.bfloat16),
                pltpu.VMEM((2 * half, TILE, TILE), jnp.bfloat16),
                pltpu.VMEM((rows, TILE), jnp.float32),
                pltpu.VMEM((half, width, TILE), jnp.float32),
                pltpu.VMEM((wide // 2, width, TILE), jnp.bfloat16),
                pltpu.VMEM((half, width, TILE), jnp.bfloat16),
                pltpu.SemaphoreType.DMA((3,)),
                pltpu.SemaphoreType.DMA((len(PIECES),)),
                pltpu.SemaphoreType.DMA((len(PIECES),)),
                pltpu.SemaphoreType.DMA,
                pltpu.SemaphoreType.DMA,
                pltpu.SemaphoreType.DMA,
                pltpu.SemaphoreType.DMA,
            ],
            compiler_params=pltpu.CompilerParams(
                collective_id=0, has_side_effects=True, vmem_limit_bytes=52 * 1024 * 1024
            ),
        )(tile_cols.T, coeffs.T, diagonal.T, tile_vals)
        return out.T

    in_specs = (
        P("narrow", "wide"),
        P("narrow", "wide"),
        P("narrow", None),
        P("narrow", None, None, None),
    )
    return jax.shard_map(
        per_device,
        mesh=mesh,
        in_specs=in_specs,
        out_specs=P("narrow", "wide"),
        check_vma=False,
    )
```

```python
import functools
import math

import jax
import jax.numpy as jnp
from jax import lax
from jax.experimental import pallas as pl
from jax.experimental.pallas import tpu as pltpu
from jax.sharding import PartitionSpec as P

MESH = pl.DeviceIdType.MESH
TILE = 128
PIECES = (5, 4, 3, 2, 1)
GROUP_SLICES = 16
GROUP_TILES = 15
ROWS = 5


def kernel(
    cols_ref,
    coeff_hbm,
    diag_hbm,
    vals_hbm,
    out_ref,
    coeff_v,
    diag_v,
    vals_v,
    x_ref,
    y_ref,
    yt_ref,
    acc_ref,
    alpha_ref,
    send_ref,
    back_ref,
    local_sem,
    pair_send,
    pair_recv,
    fwd_send,
    fwd_recv,
    ret_send,
    ret_recv,
    *,
    wide,
    scale,
):
    w = lax.axis_index("wide")
    n = lax.axis_index("narrow")
    other = 1 - n
    half = out_ref.shape[1] // TILE
    width = out_ref.shape[0]
    degree = cols_ref.shape[0]
    half_wide = wide // 2

    coeff_copy = pltpu.make_async_copy(coeff_hbm, coeff_v, local_sem.at[0])
    coeff_copy.start()
    vals_copy = pltpu.make_async_copy(vals_hbm, vals_v, local_sem.at[1])
    vals_copy.start()
    diag_copy = pltpu.make_async_copy(diag_hbm, diag_v, local_sem.at[2])
    diag_copy.start()

    barrier = pltpu.get_barrier_semaphore()

    def greet(step, carry):
        to = lax.rem(w + step, wide)

        @pl.when(step > 0)
        def _():
            pl.semaphore_signal(barrier, inc=1, device_id=(to, n), device_id_type=MESH)

        pl.semaphore_signal(barrier, inc=1, device_id=(to, other), device_id_type=MESH)
        return carry

    lax.fori_loop(0, wide, greet, 0, unroll=8)
    coeff_copy.wait()

    for i in range(half):
        x_ref[n * half + i] = coeff_v[:, i * TILE : (i + 1) * TILE].astype(jnp.bfloat16)

    pl.semaphore_wait(barrier, 2 * wide - 1)

    my_plane = lax.rem(w // 2, 2)
    side = lax.rem(my_plane + n, 2)
    quarter = half // 2
    starts = [sum(PIECES[:j]) for j in range(len(PIECES))]
    pair = []
    for j, piece in enumerate(PIECES + (quarter,)):
        if j < len(PIECES):
            part = x_ref.at[pl.ds(n * half + (1 - side) * quarter + starts[j], piece)]
        else:
            part = x_ref.at[pl.ds(n * half + side * quarter, quarter)]
        copy = pltpu.make_async_remote_copy(
            src_ref=part,
            dst_ref=part,
            send_sem=pair_send.at[j],
            recv_sem=pair_recv.at[j],
            device_id=(w, other),
            device_id_type=MESH,
        )
        copy.start()
        pair.append(copy)

    tile_half = lax.rem(w, 2)
    my_place = w // 4
    active = my_place < quarter
    slot = side * quarter + my_place

    def send_forward(from_half, place):
        tile = from_half * half + side * quarter + place
        mine = jnp.logical_and(place == my_place, from_half == tile_half)

        @pl.when(mine)
        def _():
            pltpu.make_async_copy(x_ref.at[tile], y_ref.at[w], fwd_recv).start()

        @pl.when(jnp.logical_not(mine))
        def _():
            pltpu.make_async_remote_copy(
                src_ref=x_ref.at[tile],
                dst_ref=y_ref.at[w],
                send_sem=fwd_send,
                recv_sem=fwd_recv,
                device_id=(place * 4 + my_plane * 2 + from_half, n),
                device_id_type=MESH,
            ).start()

        pltpu.make_async_remote_copy(
            src_ref=x_ref.at[tile],
            dst_ref=y_ref.at[w],
            send_sem=fwd_send,
            recv_sem=fwd_recv,
            device_id=(place * 4 + (1 - my_plane) * 2 + from_half, other),
            device_id_type=MESH,
        ).start()

    def send_own(step, carry):
        send_forward(n, lax.rem(w * 7 + step, quarter))
        return carry

    lax.fori_loop(0, quarter, send_own, 0)

    for j, piece in enumerate(PIECES):
        pair[j].wait_recv()

        def send_relayed(step, carry):
            send_forward(other, starts[j] + lax.rem(w + step, piece))
            return carry

        lax.fori_loop(0, piece, send_relayed, 0)

    vals_copy.wait()
    pair[-1].wait_recv()

    def alpha_group(group, carry):
        for u in range(ROWS):
            row = group * ROWS + u
            lhs = jnp.concatenate([x_ref[cols_ref[k, row]] for k in range(degree)], axis=1)
            rhs = jnp.concatenate([vals_v[row, k] for k in range(degree)], axis=1)
            alpha_ref[row] = lax.dot_general(
                lhs, rhs, (((1,), (1,)), ((), ())), preferred_element_type=jnp.float32
            )
        return carry

    lax.fori_loop(0, half // ROWS, alpha_group, 0)

    @pl.when(active)
    def _():
        pltpu.make_async_copy(y_ref, y_ref, fwd_recv).wait()

        def repack(g, carry):
            for t in range(GROUP_TILES):
                low, high = t * TILE, (t + 1) * TILE
                pieces = []
                while low < high:
                    source, begin = low // width, low % width
                    end = min(width, begin + high - low)
                    piece = y_ref[g * GROUP_SLICES + source].astype(jnp.float32)
                    pieces.append(piece[begin:end])
                    low += end - begin
                yt_ref[g * GROUP_TILES + t] = jnp.concatenate(pieces, axis=0).astype(
                    jnp.bfloat16
                )
            return carry

        lax.fori_loop(0, wide // GROUP_SLICES, repack, 0)

        def send_chunk(j):
            send_ref[j] = acc_ref[pl.ds(pl.multiple_of(j * width, 8), width), :].astype(
                jnp.bfloat16
            )
            to = n * half_wide + j
            mine = jnp.logical_and(to == w, tile_half == n)

            @pl.when(mine)
            def _():
                pltpu.make_async_copy(send_ref.at[j], back_ref.at[slot], ret_recv).start()

            @pl.when(jnp.logical_not(mine))
            def _():
                pltpu.make_async_remote_copy(
                    src_ref=send_ref.at[j],
                    dst_ref=back_ref.at[slot],
                    send_sem=ret_send,
                    recv_sem=ret_recv,
                    device_id=(to, tile_half),
                    device_id_type=MESH,
                ).start()

        groups = half // ROWS
        per_block = GROUP_TILES // ROWS
        first = lax.rem(w + w // 16, groups)

        def beta_group(step, carry):
            group = lax.rem(first + step, groups)
            for u in range(ROWS):
                row = group * ROWS + u
                lhs = jnp.concatenate([vals_v[row, k] for k in range(degree)], axis=1)
                rhs = jnp.concatenate([yt_ref[cols_ref[k, row]] for k in range(degree)], axis=0)
                acc_ref[pl.ds(pl.multiple_of(row * TILE, TILE), TILE), :] = jnp.dot(
                    lhs, rhs, preferred_element_type=jnp.float32
                )
            chunk = group * ROWS + group // per_block
            spot = lax.rem(group, per_block)

            @pl.when(jnp.logical_or(step > 0, spot == 0))
            def _():
                send_chunk(chunk)

            def send_rest(u, carry):
                send_chunk(chunk + u)
                return carry

            lax.fori_loop(1, jnp.where(spot == per_block - 1, ROWS + 1, ROWS), send_rest, 0)
            return carry

        lax.fori_loop(0, groups, beta_group, 0)

        @pl.when(lax.rem(first, per_block) != 0)
        def _():
            send_chunk(first * ROWS + first // per_block)

    diag_copy.wait()
    pltpu.make_async_copy(back_ref, back_ref, ret_recv).wait()

    for i in range(half):
        part = slice(i * TILE, (i + 1) * TILE)
        out_ref[:, part] = (
            scale * alpha_ref[i]
            + scale * back_ref[i].astype(jnp.float32)
            + diag_v[:, part] * coeff_v[:, part]
        )

    for copy in pair:
        copy.wait_send()

    @pl.when(active)
    def _():
        done = x_ref.at[pl.ds(0, 2 * half - 1)]
        pltpu.make_async_copy(done, done, fwd_send).wait()

    @pl.when(jnp.logical_not(active))
    def _():
        pltpu.make_async_copy(x_ref, x_ref, fwd_send).wait()

    own_return = jnp.logical_and(tile_half == n, w // half_wide == n)

    @pl.when(jnp.logical_and(active, own_return))
    def _():
        done = send_ref.at[pl.ds(0, half_wide - 1)]
        pltpu.make_async_copy(done, done, ret_send).wait()

    @pl.when(jnp.logical_and(active, jnp.logical_not(own_return)))
    def _():
        pltpu.make_async_copy(send_ref, send_ref, ret_send).wait()


def solution(mesh):
    wide = mesh.shape["wide"]

    def per_device(coeffs, diagonal, tile_cols, tile_vals):
        rows, width = coeffs.shape
        half, degree = tile_cols.shape
        scale = 1.0 / math.sqrt(degree * TILE)
        any_space = pl.BlockSpec(memory_space=pl.ANY)
        out = pl.pallas_call(
            functools.partial(kernel, wide=wide, scale=scale),
            out_shape=jax.ShapeDtypeStruct((width, rows), jnp.float32),
            in_specs=[
                pl.BlockSpec(memory_space=pltpu.SMEM),
                any_space,
                any_space,
                any_space,
            ],
            out_specs=pl.BlockSpec(memory_space=pltpu.VMEM),
            scratch_shapes=[
                pltpu.VMEM((width, rows), jnp.float32),
                pltpu.VMEM((width, rows), jnp.float32),
                pltpu.VMEM((half, degree, TILE, TILE), jnp.bfloat16),
                pltpu.VMEM((2 * half, width, TILE), jnp.bfloat16),
                pltpu.VMEM((wide, width, TILE), jnp.bfloat16),
                pltpu.VMEM((2 * half, TILE, TILE), jnp.bfloat16),
                pltpu.VMEM((rows, TILE), jnp.float32),
                pltpu.VMEM((half, width, TILE), jnp.float32),
                pltpu.VMEM((wide // 2, width, TILE), jnp.bfloat16),
                pltpu.VMEM((half, width, TILE), jnp.bfloat16),
                pltpu.SemaphoreType.DMA((3,)),
                pltpu.SemaphoreType.DMA((len(PIECES) + 1,)),
                pltpu.SemaphoreType.DMA((len(PIECES) + 1,)),
                pltpu.SemaphoreType.DMA,
                pltpu.SemaphoreType.DMA,
                pltpu.SemaphoreType.DMA,
                pltpu.SemaphoreType.DMA,
            ],
            compiler_params=pltpu.CompilerParams(
                collective_id=0, has_side_effects=True, vmem_limit_bytes=52 * 1024 * 1024
            ),
        )(tile_cols.T, coeffs.T, diagonal.T, tile_vals)
        return out.T

    in_specs = (
        P("narrow", "wide"),
        P("narrow", "wide"),
        P("narrow", None),
        P("narrow", None, None, None),
    )
    return jax.shard_map(
        per_device,
        mesh=mesh,
        in_specs=in_specs,
        out_specs=P("narrow", "wide"),
        check_vma=False,
    )
```

```python
import functools
import math

import jax
import jax.numpy as jnp
from jax import lax
from jax.experimental import pallas as pl
from jax.experimental.pallas import tpu as pltpu
from jax.sharding import PartitionSpec as P

MESH = pl.DeviceIdType.MESH
TILE = 128
PIECES = (5, 4, 3, 2, 1)
GROUP_SLICES = 16
GROUP_TILES = 15
ROWS = 5


def kernel(
    cols_hbm,
    coeff_hbm,
    diag_hbm,
    vals_hbm,
    out_ref,
    cols_ref,
    coeff_v,
    diag_v,
    vals_v,
    x_ref,
    y_ref,
    yt_ref,
    acc_ref,
    alpha_ref,
    send_ref,
    back_ref,
    local_sem,
    pair_send,
    pair_recv,
    fwd_send,
    fwd_recv,
    ret_send,
    ret_recv,
    *,
    wide,
    scale,
):
    w = lax.axis_index("wide")
    n = lax.axis_index("narrow")
    other = 1 - n
    half = out_ref.shape[1] // TILE
    width = out_ref.shape[0]
    degree = cols_ref.shape[0]
    half_wide = wide // 2

    coeff_copy = pltpu.make_async_copy(coeff_hbm, coeff_v, local_sem.at[0])
    coeff_copy.start()
    vals_copy = pltpu.make_async_copy(vals_hbm, vals_v, local_sem.at[1])
    vals_copy.start()
    diag_copy = pltpu.make_async_copy(diag_hbm, diag_v, local_sem.at[2])
    diag_copy.start()
    cols_copy = pltpu.make_async_copy(cols_hbm, cols_ref, local_sem.at[3])
    cols_copy.start()

    barrier = pltpu.get_barrier_semaphore()

    def greet(step, carry):
        to = lax.rem(w + step, wide)

        @pl.when(step > 0)
        def _():
            pl.semaphore_signal(barrier, inc=1, device_id=(to, n), device_id_type=MESH)

        pl.semaphore_signal(barrier, inc=1, device_id=(to, other), device_id_type=MESH)
        return carry

    lax.fori_loop(0, wide, greet, 0, unroll=8)
    coeff_copy.wait()

    for i in range(half):
        x_ref[n * half + i] = coeff_v[:, i * TILE : (i + 1) * TILE].astype(jnp.bfloat16)

    pl.semaphore_wait(barrier, 2 * wide - 1)

    my_plane = lax.rem(w // 2, 2)
    side = lax.rem(my_plane + n, 2)
    quarter = half // 2
    starts = [sum(PIECES[:j]) for j in range(len(PIECES))]
    pair = []
    for j, piece in enumerate(PIECES + (quarter,)):
        if j < len(PIECES):
            part = x_ref.at[pl.ds(n * half + (1 - side) * quarter + starts[j], piece)]
        else:
            part = x_ref.at[pl.ds(n * half + side * quarter, quarter)]
        copy = pltpu.make_async_remote_copy(
            src_ref=part,
            dst_ref=part,
            send_sem=pair_send.at[j],
            recv_sem=pair_recv.at[j],
            device_id=(w, other),
            device_id_type=MESH,
        )
        copy.start()
        pair.append(copy)

    tile_half = lax.rem(w + my_plane, 2)
    my_place = w // 4
    active = my_place < quarter
    slot = side * quarter + my_place

    def send_forward(from_half, place):
        tile = from_half * half + side * quarter + place
        mine = jnp.logical_and(place == my_place, from_half == tile_half)

        @pl.when(mine)
        def _():
            pltpu.make_async_copy(x_ref.at[tile], y_ref.at[w], fwd_recv).start()

        @pl.when(jnp.logical_not(mine))
        def _():
            pltpu.make_async_remote_copy(
                src_ref=x_ref.at[tile],
                dst_ref=y_ref.at[w],
                send_sem=fwd_send,
                recv_sem=fwd_recv,
                device_id=(place * 4 + my_plane * 2 + lax.rem(from_half + my_plane, 2), n),
                device_id_type=MESH,
            ).start()

        pltpu.make_async_remote_copy(
            src_ref=x_ref.at[tile],
            dst_ref=y_ref.at[w],
            send_sem=fwd_send,
            recv_sem=fwd_recv,
            device_id=(
                place * 4 + (1 - my_plane) * 2 + lax.rem(from_half + 1 - my_plane, 2),
                other,
            ),
            device_id_type=MESH,
        ).start()

    def send_own(step, carry):
        send_forward(n, lax.rem(w * 7 + step, quarter))
        return carry

    lax.fori_loop(0, quarter, send_own, 0)

    for j, piece in enumerate(PIECES):
        pair[j].wait_recv()

        def send_relayed(step, carry):
            send_forward(other, starts[j] + lax.rem(w + step, piece))
            return carry

        lax.fori_loop(0, piece, send_relayed, 0)

    vals_copy.wait()
    cols_copy.wait()

    @pl.when(active)
    def _():
        pltpu.make_async_copy(y_ref, y_ref, fwd_recv).wait()

        def repack(g, carry):
            for t in range(GROUP_TILES):
                low, high = t * TILE, (t + 1) * TILE
                pieces = []
                while low < high:
                    source, begin = low // width, low % width
                    end = min(width, begin + high - low)
                    piece = y_ref[g * GROUP_SLICES + source].astype(jnp.float32)
                    pieces.append(piece[begin:end])
                    low += end - begin
                yt_ref[g * GROUP_TILES + t] = jnp.concatenate(pieces, axis=0).astype(
                    jnp.bfloat16
                )
            return carry

        lax.fori_loop(0, wide // GROUP_SLICES, repack, 0)

        def send_chunk(j):
            send_ref[j] = acc_ref[pl.ds(pl.multiple_of(j * width, 8), width), :].astype(
                jnp.bfloat16
            )
            to = n * half_wide + j
            mine = jnp.logical_and(to == w, tile_half == n)

            @pl.when(mine)
            def _():
                pltpu.make_async_copy(send_ref.at[j], back_ref.at[slot], ret_recv).start()

            @pl.when(jnp.logical_not(mine))
            def _():
                pltpu.make_async_remote_copy(
                    src_ref=send_ref.at[j],
                    dst_ref=back_ref.at[slot],
                    send_sem=ret_send,
                    recv_sem=ret_recv,
                    device_id=(to, tile_half),
                    device_id_type=MESH,
                ).start()

        groups = half // ROWS
        per_block = GROUP_TILES // ROWS
        first = lax.rem(w + w // 16, groups)

        def beta_group(step, carry):
            group = lax.rem(first + step, groups)
            for u in range(ROWS):
                row = group * ROWS + u
                lhs = jnp.concatenate([vals_v[row, k] for k in range(degree)], axis=1)
                rhs = jnp.concatenate([yt_ref[cols_ref[k, row]] for k in range(degree)], axis=0)
                acc_ref[pl.ds(pl.multiple_of(row * TILE, TILE), TILE), :] = jnp.dot(
                    lhs, rhs, preferred_element_type=jnp.float32
                )
            chunk = group * ROWS + group // per_block
            spot = lax.rem(group, per_block)

            @pl.when(jnp.logical_or(step > 0, spot == 0))
            def _():
                send_chunk(chunk)

            def send_rest(u, carry):
                send_chunk(chunk + u)
                return carry

            lax.fori_loop(1, jnp.where(spot == per_block - 1, ROWS + 1, ROWS), send_rest, 0)
            return carry

        lax.fori_loop(0, groups, beta_group, 0)

        @pl.when(lax.rem(first, per_block) != 0)
        def _():
            send_chunk(first * ROWS + first // per_block)

    pair[-1].wait_recv()

    def alpha_group(group, carry):
        for u in range(ROWS):
            row = group * ROWS + u
            lhs = jnp.concatenate([x_ref[cols_ref[k, row]] for k in range(degree)], axis=1)
            rhs = jnp.concatenate([vals_v[row, k] for k in range(degree)], axis=1)
            alpha_ref[row] = lax.dot_general(
                lhs, rhs, (((1,), (1,)), ((), ())), preferred_element_type=jnp.float32
            )
        return carry

    lax.fori_loop(0, half // ROWS, alpha_group, 0)

    diag_copy.wait()
    for i in range(half):
        part = slice(i * TILE, (i + 1) * TILE)
        out_ref[:, part] = scale * alpha_ref[i] + diag_v[:, part] * coeff_v[:, part]

    pltpu.make_async_copy(back_ref, back_ref, ret_recv).wait()
    for i in range(half):
        part = slice(i * TILE, (i + 1) * TILE)
        out_ref[:, part] += scale * back_ref[i].astype(jnp.float32)

    for copy in pair:
        copy.wait_send()

    @pl.when(active)
    def _():
        done = x_ref.at[pl.ds(0, 2 * half - 1)]
        pltpu.make_async_copy(done, done, fwd_send).wait()

    @pl.when(jnp.logical_not(active))
    def _():
        pltpu.make_async_copy(x_ref, x_ref, fwd_send).wait()

    own_return = jnp.logical_and(tile_half == n, w // half_wide == n)

    @pl.when(jnp.logical_and(active, own_return))
    def _():
        done = send_ref.at[pl.ds(0, half_wide - 1)]
        pltpu.make_async_copy(done, done, ret_send).wait()

    @pl.when(jnp.logical_and(active, jnp.logical_not(own_return)))
    def _():
        pltpu.make_async_copy(send_ref, send_ref, ret_send).wait()


def solution(mesh):
    wide = mesh.shape["wide"]

    def per_device(coeffs, diagonal, tile_cols, tile_vals):
        rows, width = coeffs.shape
        half, degree = tile_cols.shape
        scale = 1.0 / math.sqrt(degree * TILE)
        any_space = pl.BlockSpec(memory_space=pl.ANY)
        out = pl.pallas_call(
            functools.partial(kernel, wide=wide, scale=scale),
            out_shape=jax.ShapeDtypeStruct((width, rows), jnp.float32),
            in_specs=[
                any_space,
                any_space,
                any_space,
                any_space,
            ],
            out_specs=pl.BlockSpec(memory_space=pltpu.VMEM),
            scratch_shapes=[
                pltpu.SMEM((degree, half), jnp.int32),
                pltpu.VMEM((width, rows), jnp.float32),
                pltpu.VMEM((width, rows), jnp.float32),
                pltpu.VMEM((half, degree, TILE, TILE), jnp.bfloat16),
                pltpu.VMEM((2 * half, width, TILE), jnp.bfloat16),
                pltpu.VMEM((wide, width, TILE), jnp.bfloat16),
                pltpu.VMEM((2 * half, TILE, TILE), jnp.bfloat16),
                pltpu.VMEM((rows, TILE), jnp.float32),
                pltpu.VMEM((half, width, TILE), jnp.float32),
                pltpu.VMEM((wide // 2, width, TILE), jnp.bfloat16),
                pltpu.VMEM((half, width, TILE), jnp.bfloat16),
                pltpu.SemaphoreType.DMA((4,)),
                pltpu.SemaphoreType.DMA((len(PIECES) + 1,)),
                pltpu.SemaphoreType.DMA((len(PIECES) + 1,)),
                pltpu.SemaphoreType.DMA,
                pltpu.SemaphoreType.DMA,
                pltpu.SemaphoreType.DMA,
                pltpu.SemaphoreType.DMA,
            ],
            compiler_params=pltpu.CompilerParams(
                collective_id=0, has_side_effects=True, vmem_limit_bytes=52 * 1024 * 1024
            ),
        )(tile_cols.T, coeffs.T, diagonal.T, tile_vals)
        return out.T

    in_specs = (
        P("narrow", "wide"),
        P("narrow", "wide"),
        P("narrow", None),
        P("narrow", None, None, None),
    )
    return jax.shard_map(
        per_device,
        mesh=mesh,
        in_specs=in_specs,
        out_specs=P("narrow", "wide"),
        check_vma=False,
    )
```

```python
import functools
import math

import jax
import jax.numpy as jnp
from jax import lax
from jax.experimental import pallas as pl
from jax.experimental.pallas import tpu as pltpu
from jax.sharding import PartitionSpec as P

MESH = pl.DeviceIdType.MESH
TILE = 128
PIECES = (5, 4, 3, 2, 1)
GROUP_SLICES = 16
GROUP_TILES = 15
ROWS = 5


def kernel(
    cols_hbm,
    coeff_hbm,
    diag_hbm,
    vals_hbm,
    out_ref,
    cols_ref,
    coeff_v,
    diag_v,
    vals_v,
    x_ref,
    y_ref,
    yt_ref,
    acc_ref,
    alpha_ref,
    send_ref,
    back_ref,
    local_sem,
    pair_send,
    pair_recv,
    fwd_send,
    fwd_recv,
    ret_send,
    ret_recv,
    *,
    wide,
    scale,
):
    w = lax.axis_index("wide")
    n = lax.axis_index("narrow")
    other = 1 - n
    half = out_ref.shape[1] // TILE
    width = out_ref.shape[0]
    degree = cols_ref.shape[0]
    half_wide = wide // 2

    coeff_copy = pltpu.make_async_copy(coeff_hbm, coeff_v, local_sem.at[0])
    coeff_copy.start()

    barrier = pltpu.get_barrier_semaphore()

    def greet(step, carry):
        to = lax.rem(w + step, wide)

        @pl.when(step > 0)
        def _():
            pl.semaphore_signal(barrier, inc=1, device_id=(to, n), device_id_type=MESH)

        pl.semaphore_signal(barrier, inc=1, device_id=(to, other), device_id_type=MESH)
        return carry

    lax.fori_loop(0, wide, greet, 0, unroll=8)
    coeff_copy.wait()
    vals_copy = pltpu.make_async_copy(vals_hbm, vals_v, local_sem.at[1])
    vals_copy.start()
    diag_copy = pltpu.make_async_copy(diag_hbm, diag_v, local_sem.at[2])
    diag_copy.start()
    cols_copy = pltpu.make_async_copy(cols_hbm, cols_ref, local_sem.at[3])
    cols_copy.start()

    for i in range(half):
        x_ref[n * half + i] = coeff_v[:, i * TILE : (i + 1) * TILE].astype(jnp.bfloat16)

    pl.semaphore_wait(barrier, 2 * wide - 1)

    my_plane = lax.rem(w // 2, 2)
    side = lax.rem(my_plane + n, 2)
    quarter = half // 2
    starts = [sum(PIECES[:j]) for j in range(len(PIECES))]
    pair = []
    for j, piece in enumerate(PIECES + (quarter,)):
        if j < len(PIECES):
            part = x_ref.at[pl.ds(n * half + (1 - side) * quarter + starts[j], piece)]
        else:
            part = x_ref.at[pl.ds(n * half + side * quarter, quarter)]
        copy = pltpu.make_async_remote_copy(
            src_ref=part,
            dst_ref=part,
            send_sem=pair_send.at[j],
            recv_sem=pair_recv.at[j],
            device_id=(w, other),
            device_id_type=MESH,
        )
        if j < len(PIECES):
            copy.start()
        pair.append(copy)

    tile_half = lax.rem(w + my_plane, 2)
    my_place = w // 4
    active = my_place < quarter
    slot = side * quarter + my_place

    def send_forward(from_half, place):
        tile = from_half * half + side * quarter + place
        mine = jnp.logical_and(place == my_place, from_half == tile_half)

        @pl.when(mine)
        def _():
            pltpu.make_async_copy(x_ref.at[tile], y_ref.at[w], fwd_recv).start()

        @pl.when(jnp.logical_not(mine))
        def _():
            pltpu.make_async_remote_copy(
                src_ref=x_ref.at[tile],
                dst_ref=y_ref.at[w],
                send_sem=fwd_send,
                recv_sem=fwd_recv,
                device_id=(place * 4 + my_plane * 2 + lax.rem(from_half + my_plane, 2), n),
                device_id_type=MESH,
            ).start()

        pltpu.make_async_remote_copy(
            src_ref=x_ref.at[tile],
            dst_ref=y_ref.at[w],
            send_sem=fwd_send,
            recv_sem=fwd_recv,
            device_id=(
                place * 4 + (1 - my_plane) * 2 + lax.rem(from_half + 1 - my_plane, 2),
                other,
            ),
            device_id_type=MESH,
        ).start()

    def send_own(step, carry):
        send_forward(n, lax.rem(w * 7 + step, quarter))
        return carry

    lax.fori_loop(0, quarter, send_own, 0)

    for j, piece in enumerate(PIECES):
        pair[j].wait_recv()

        def send_relayed(step, carry):
            send_forward(other, starts[j] + lax.rem(w + step, piece))
            return carry

        lax.fori_loop(0, piece, send_relayed, 0)

    pair[-1].start()

    vals_copy.wait()
    cols_copy.wait()

    @pl.when(active)
    def _():
        pltpu.make_async_copy(y_ref, y_ref, fwd_recv).wait()

        def repack(g, carry):
            for t in range(GROUP_TILES):
                low, high = t * TILE, (t + 1) * TILE
                pieces = []
                while low < high:
                    source, begin = low // width, low % width
                    end = min(width, begin + high - low)
                    piece = y_ref[g * GROUP_SLICES + source].astype(jnp.float32)
                    pieces.append(piece[begin:end])
                    low += end - begin
                yt_ref[g * GROUP_TILES + t] = jnp.concatenate(pieces, axis=0).astype(
                    jnp.bfloat16
                )
            return carry

        lax.fori_loop(0, wide // GROUP_SLICES, repack, 0)

        def send_chunk(j):
            send_ref[j] = acc_ref[pl.ds(pl.multiple_of(j * width, 8), width), :].astype(
                jnp.bfloat16
            )
            to = n * half_wide + j
            mine = jnp.logical_and(to == w, tile_half == n)

            @pl.when(mine)
            def _():
                pltpu.make_async_copy(send_ref.at[j], back_ref.at[slot], ret_recv).start()

            @pl.when(jnp.logical_not(mine))
            def _():
                pltpu.make_async_remote_copy(
                    src_ref=send_ref.at[j],
                    dst_ref=back_ref.at[slot],
                    send_sem=ret_send,
                    recv_sem=ret_recv,
                    device_id=(to, tile_half),
                    device_id_type=MESH,
                ).start()

        groups = half // ROWS
        per_block = GROUP_TILES // ROWS
        number = lax.rem(my_place * 7 + my_plane * 15, half)
        first = lax.rem(number, groups)
        turn = number // groups

        def beta_group(step, carry):
            group = lax.rem(first + step, groups)
            for u in range(ROWS):
                row = group * ROWS + u
                lhs = jnp.concatenate([vals_v[row, k] for k in range(degree)], axis=1)
                rhs = jnp.concatenate([yt_ref[cols_ref[k, row]] for k in range(degree)], axis=0)
                acc_ref[pl.ds(pl.multiple_of(row * TILE, TILE), TILE), :] = jnp.dot(
                    lhs, rhs, preferred_element_type=jnp.float32
                )
            chunk = group * ROWS + group // per_block
            spot = lax.rem(group, per_block)

            def send_one(i, carry):
                u = lax.rem(turn + i, ROWS)

                @pl.when(jnp.logical_or(step + u > 0, spot == 0))
                def _():
                    send_chunk(chunk + u)

                return carry

            lax.fori_loop(0, ROWS, send_one, 0)

            @pl.when(spot == per_block - 1)
            def _():
                send_chunk(chunk + ROWS)

            return carry

        lax.fori_loop(0, groups, beta_group, 0)

        @pl.when(lax.rem(first, per_block) != 0)
        def _():
            send_chunk(first * ROWS + first // per_block)

    pair[-1].wait_recv()

    def alpha_group(group, carry):
        for u in range(ROWS):
            row = group * ROWS + u
            lhs = jnp.concatenate([x_ref[cols_ref[k, row]] for k in range(degree)], axis=1)
            rhs = jnp.concatenate([vals_v[row, k] for k in range(degree)], axis=1)
            alpha_ref[row] = lax.dot_general(
                lhs, rhs, (((1,), (1,)), ((), ())), preferred_element_type=jnp.float32
            )
        return carry

    lax.fori_loop(0, half // ROWS, alpha_group, 0)

    diag_copy.wait()
    for i in range(half):
        part = slice(i * TILE, (i + 1) * TILE)
        out_ref[:, part] = scale * alpha_ref[i] + diag_v[:, part] * coeff_v[:, part]

    pltpu.make_async_copy(back_ref, back_ref, ret_recv).wait()
    for i in range(half):
        part = slice(i * TILE, (i + 1) * TILE)
        out_ref[:, part] += scale * back_ref[i].astype(jnp.float32)

    for copy in pair:
        copy.wait_send()

    @pl.when(active)
    def _():
        done = x_ref.at[pl.ds(0, 2 * half - 1)]
        pltpu.make_async_copy(done, done, fwd_send).wait()

    @pl.when(jnp.logical_not(active))
    def _():
        pltpu.make_async_copy(x_ref, x_ref, fwd_send).wait()

    own_return = jnp.logical_and(tile_half == n, w // half_wide == n)

    @pl.when(jnp.logical_and(active, own_return))
    def _():
        done = send_ref.at[pl.ds(0, half_wide - 1)]
        pltpu.make_async_copy(done, done, ret_send).wait()

    @pl.when(jnp.logical_and(active, jnp.logical_not(own_return)))
    def _():
        pltpu.make_async_copy(send_ref, send_ref, ret_send).wait()


def solution(mesh):
    wide = mesh.shape["wide"]

    def per_device(coeffs, diagonal, tile_cols, tile_vals):
        rows, width = coeffs.shape
        half, degree = tile_cols.shape
        scale = 1.0 / math.sqrt(degree * TILE)
        any_space = pl.BlockSpec(memory_space=pl.ANY)
        out = pl.pallas_call(
            functools.partial(kernel, wide=wide, scale=scale),
            out_shape=jax.ShapeDtypeStruct((width, rows), jnp.float32),
            in_specs=[
                any_space,
                any_space,
                any_space,
                any_space,
            ],
            out_specs=pl.BlockSpec(memory_space=pltpu.VMEM),
            scratch_shapes=[
                pltpu.SMEM((degree, half), jnp.int32),
                pltpu.VMEM((width, rows), jnp.float32),
                pltpu.VMEM((width, rows), jnp.float32),
                pltpu.VMEM((half, degree, TILE, TILE), jnp.bfloat16),
                pltpu.VMEM((2 * half, width, TILE), jnp.bfloat16),
                pltpu.VMEM((wide, width, TILE), jnp.bfloat16),
                pltpu.VMEM((2 * half, TILE, TILE), jnp.bfloat16),
                pltpu.VMEM((rows, TILE), jnp.float32),
                pltpu.VMEM((half, width, TILE), jnp.float32),
                pltpu.VMEM((wide // 2, width, TILE), jnp.bfloat16),
                pltpu.VMEM((half, width, TILE), jnp.bfloat16),
                pltpu.SemaphoreType.DMA((4,)),
                pltpu.SemaphoreType.DMA((len(PIECES) + 1,)),
                pltpu.SemaphoreType.DMA((len(PIECES) + 1,)),
                pltpu.SemaphoreType.DMA,
                pltpu.SemaphoreType.DMA,
                pltpu.SemaphoreType.DMA,
                pltpu.SemaphoreType.DMA,
            ],
            compiler_params=pltpu.CompilerParams(
                collective_id=0, has_side_effects=True, vmem_limit_bytes=52 * 1024 * 1024
            ),
        )(tile_cols.T, coeffs.T, diagonal.T, tile_vals)
        return out.T

    in_specs = (
        P("narrow", "wide"),
        P("narrow", "wide"),
        P("narrow", None),
        P("narrow", None, None, None),
    )
    return jax.shard_map(
        per_device,
        mesh=mesh,
        in_specs=in_specs,
        out_specs=P("narrow", "wide"),
        check_vma=False,
    )
```

```python
import functools
import math

import jax
import jax.numpy as jnp
from jax import lax
from jax.experimental import pallas as pl
from jax.experimental.pallas import tpu as pltpu
from jax.sharding import PartitionSpec as P

MESH = pl.DeviceIdType.MESH
TILE = 128
PIECES = (5, 4, 3, 2, 1)
GROUP_SLICES = 16
GROUP_TILES = 15
ROWS = 5


def kernel(
    cols_hbm,
    coeff_hbm,
    diag_hbm,
    vals_hbm,
    out_ref,
    cols_ref,
    coeff_v,
    diag_v,
    vals_v,
    x_ref,
    y_ref,
    yt_ref,
    acc_ref,
    alpha_ref,
    send_ref,
    back_ref,
    local_sem,
    pair_send,
    pair_recv,
    fwd_send,
    fwd_recv,
    ret_send,
    ret_recv,
    *,
    wide,
    scale,
):
    w = lax.axis_index("wide")
    n = lax.axis_index("narrow")
    other = 1 - n
    half = out_ref.shape[1] // TILE
    width = out_ref.shape[0]
    degree = cols_ref.shape[0]
    half_wide = wide // 2

    coeff_copy = pltpu.make_async_copy(coeff_hbm, coeff_v, local_sem.at[0])
    coeff_copy.start()
    vals_copy = pltpu.make_async_copy(vals_hbm, vals_v, local_sem.at[1])
    vals_copy.start()
    diag_copy = pltpu.make_async_copy(diag_hbm, diag_v, local_sem.at[2])
    diag_copy.start()
    cols_copy = pltpu.make_async_copy(cols_hbm, cols_ref, local_sem.at[3])
    cols_copy.start()

    barrier = pltpu.get_barrier_semaphore()

    def greet(step, carry):
        to = lax.rem(w + step, wide)

        @pl.when(step > 0)
        def _():
            pl.semaphore_signal(barrier, inc=1, device_id=(to, n), device_id_type=MESH)

        pl.semaphore_signal(barrier, inc=1, device_id=(to, other), device_id_type=MESH)
        return carry

    lax.fori_loop(0, wide, greet, 0, unroll=8)
    coeff_copy.wait()

    for i in range(half):
        x_ref[n * half + i] = coeff_v[:, i * TILE : (i + 1) * TILE].astype(jnp.bfloat16)

    pl.semaphore_wait(barrier, 2 * wide - 1)

    my_plane = lax.rem(w // 2, 2)
    side = lax.rem(my_plane + n, 2)
    quarter = half // 2
    starts = [sum(PIECES[:j]) for j in range(len(PIECES))]
    pair = []
    for j, piece in enumerate(PIECES + (quarter,)):
        if j < len(PIECES):
            part = x_ref.at[pl.ds(n * half + (1 - side) * quarter + starts[j], piece)]
        else:
            part = x_ref.at[pl.ds(n * half + side * quarter, quarter)]
        copy = pltpu.make_async_remote_copy(
            src_ref=part,
            dst_ref=part,
            send_sem=pair_send.at[j],
            recv_sem=pair_recv.at[j],
            device_id=(w, other),
            device_id_type=MESH,
        )
        copy.start()
        pair.append(copy)

    my_place = w // 4
    tile_half = lax.rem(w + my_plane + my_place, 2)
    active = my_place < quarter
    slot = side * quarter + my_place

    def send_forward(from_half, place):
        tile = from_half * half + side * quarter + place
        mine = jnp.logical_and(place == my_place, from_half == tile_half)

        @pl.when(mine)
        def _():
            pltpu.make_async_copy(x_ref.at[tile], y_ref.at[w], fwd_recv).start()

        @pl.when(jnp.logical_not(mine))
        def _():
            pltpu.make_async_remote_copy(
                src_ref=x_ref.at[tile],
                dst_ref=y_ref.at[w],
                send_sem=fwd_send,
                recv_sem=fwd_recv,
                device_id=(place * 4 + my_plane * 2 + lax.rem(from_half + my_plane + place, 2), n),
                device_id_type=MESH,
            ).start()

        pltpu.make_async_remote_copy(
            src_ref=x_ref.at[tile],
            dst_ref=y_ref.at[w],
            send_sem=fwd_send,
            recv_sem=fwd_recv,
            device_id=(
                place * 4 + (1 - my_plane) * 2 + lax.rem(from_half + 1 - my_plane + place, 2),
                other,
            ),
            device_id_type=MESH,
        ).start()

    def send_own(step, carry):
        send_forward(n, lax.rem(w * 7 + step, quarter))
        return carry

    lax.fori_loop(0, quarter, send_own, 0)

    for j, piece in enumerate(PIECES):
        pair[j].wait_recv()

        def send_relayed(step, carry):
            send_forward(other, starts[j] + lax.rem(w + step, piece))
            return carry

        lax.fori_loop(0, piece, send_relayed, 0)

    vals_copy.wait()
    cols_copy.wait()

    @pl.when(active)
    def _():
        pltpu.make_async_copy(y_ref, y_ref, fwd_recv).wait()

        def repack(g, carry):
            for t in range(GROUP_TILES):
                low, high = t * TILE, (t + 1) * TILE
                pieces = []
                while low < high:
                    source, begin = low // width, low % width
                    end = min(width, begin + high - low)
                    piece = y_ref[g * GROUP_SLICES + source].astype(jnp.float32)
                    pieces.append(piece[begin:end])
                    low += end - begin
                yt_ref[g * GROUP_TILES + t] = jnp.concatenate(pieces, axis=0).astype(
                    jnp.bfloat16
                )
            return carry

        lax.fori_loop(0, wide // GROUP_SLICES, repack, 0)

        def send_chunk(j):
            send_ref[j] = acc_ref[pl.ds(pl.multiple_of(j * width, 8), width), :].astype(
                jnp.bfloat16
            )
            to = n * half_wide + j
            mine = jnp.logical_and(to == w, tile_half == n)

            @pl.when(mine)
            def _():
                pltpu.make_async_copy(send_ref.at[j], back_ref.at[slot], ret_recv).start()

            @pl.when(jnp.logical_not(mine))
            def _():
                pltpu.make_async_remote_copy(
                    src_ref=send_ref.at[j],
                    dst_ref=back_ref.at[slot],
                    send_sem=ret_send,
                    recv_sem=ret_recv,
                    device_id=(to, tile_half),
                    device_id_type=MESH,
                ).start()

        groups = half // ROWS
        per_block = GROUP_TILES // ROWS
        first = lax.rem(w + w // 16, groups)

        def beta_group(step, carry):
            group = lax.rem(first + step, groups)
            for u in range(ROWS):
                row = group * ROWS + u
                lhs = jnp.concatenate([vals_v[row, k] for k in range(degree)], axis=1)
                rhs = jnp.concatenate([yt_ref[cols_ref[k, row]] for k in range(degree)], axis=0)
                acc_ref[pl.ds(pl.multiple_of(row * TILE, TILE), TILE), :] = jnp.dot(
                    lhs, rhs, preferred_element_type=jnp.float32
                )
            chunk = group * ROWS + group // per_block
            spot = lax.rem(group, per_block)

            @pl.when(jnp.logical_or(step > 0, spot == 0))
            def _():
                send_chunk(chunk)

            def send_rest(u, carry):
                send_chunk(chunk + u)
                return carry

            lax.fori_loop(1, jnp.where(spot == per_block - 1, ROWS + 1, ROWS), send_rest, 0)
            return carry

        lax.fori_loop(0, groups, beta_group, 0)

        @pl.when(lax.rem(first, per_block) != 0)
        def _():
            send_chunk(first * ROWS + first // per_block)

    pair[-1].wait_recv()

    def alpha_group(group, carry):
        for u in range(ROWS):
            row = group * ROWS + u
            lhs = jnp.concatenate([x_ref[cols_ref[k, row]] for k in range(degree)], axis=1)
            rhs = jnp.concatenate([vals_v[row, k] for k in range(degree)], axis=1)
            alpha_ref[row] = lax.dot_general(
                lhs, rhs, (((1,), (1,)), ((), ())), preferred_element_type=jnp.float32
            )
        return carry

    lax.fori_loop(0, half // ROWS, alpha_group, 0)

    diag_copy.wait()
    for i in range(half):
        part = slice(i * TILE, (i + 1) * TILE)
        out_ref[:, part] = scale * alpha_ref[i] + diag_v[:, part] * coeff_v[:, part]

    pltpu.make_async_copy(back_ref, back_ref, ret_recv).wait()
    for i in range(half):
        part = slice(i * TILE, (i + 1) * TILE)
        out_ref[:, part] += scale * back_ref[i].astype(jnp.float32)

    for copy in pair:
        copy.wait_send()

    @pl.when(active)
    def _():
        done = x_ref.at[pl.ds(0, 2 * half - 1)]
        pltpu.make_async_copy(done, done, fwd_send).wait()

    @pl.when(jnp.logical_not(active))
    def _():
        pltpu.make_async_copy(x_ref, x_ref, fwd_send).wait()

    own_return = jnp.logical_and(tile_half == n, w // half_wide == n)

    @pl.when(jnp.logical_and(active, own_return))
    def _():
        done = send_ref.at[pl.ds(0, half_wide - 1)]
        pltpu.make_async_copy(done, done, ret_send).wait()

    @pl.when(jnp.logical_and(active, jnp.logical_not(own_return)))
    def _():
        pltpu.make_async_copy(send_ref, send_ref, ret_send).wait()


def solution(mesh):
    wide = mesh.shape["wide"]

    def per_device(coeffs, diagonal, tile_cols, tile_vals):
        rows, width = coeffs.shape
        half, degree = tile_cols.shape
        scale = 1.0 / math.sqrt(degree * TILE)
        any_space = pl.BlockSpec(memory_space=pl.ANY)
        out = pl.pallas_call(
            functools.partial(kernel, wide=wide, scale=scale),
            out_shape=jax.ShapeDtypeStruct((width, rows), jnp.float32),
            in_specs=[
                any_space,
                any_space,
                any_space,
                any_space,
            ],
            out_specs=pl.BlockSpec(memory_space=pltpu.VMEM),
            scratch_shapes=[
                pltpu.SMEM((degree, half), jnp.int32),
                pltpu.VMEM((width, rows), jnp.float32),
                pltpu.VMEM((width, rows), jnp.float32),
                pltpu.VMEM((half, degree, TILE, TILE), jnp.bfloat16),
                pltpu.VMEM((2 * half, width, TILE), jnp.bfloat16),
                pltpu.VMEM((wide, width, TILE), jnp.bfloat16),
                pltpu.VMEM((2 * half, TILE, TILE), jnp.bfloat16),
                pltpu.VMEM((rows, TILE), jnp.float32),
                pltpu.VMEM((half, width, TILE), jnp.float32),
                pltpu.VMEM((wide // 2, width, TILE), jnp.bfloat16),
                pltpu.VMEM((half, width, TILE), jnp.bfloat16),
                pltpu.SemaphoreType.DMA((4,)),
                pltpu.SemaphoreType.DMA((len(PIECES) + 1,)),
                pltpu.SemaphoreType.DMA((len(PIECES) + 1,)),
                pltpu.SemaphoreType.DMA,
                pltpu.SemaphoreType.DMA,
                pltpu.SemaphoreType.DMA,
                pltpu.SemaphoreType.DMA,
            ],
            compiler_params=pltpu.CompilerParams(
                collective_id=0, has_side_effects=True, vmem_limit_bytes=52 * 1024 * 1024
            ),
        )(tile_cols.T, coeffs.T, diagonal.T, tile_vals)
        return out.T

    in_specs = (
        P("narrow", "wide"),
        P("narrow", "wide"),
        P("narrow", None),
        P("narrow", None, None, None),
    )
    return jax.shard_map(
        per_device,
        mesh=mesh,
        in_specs=in_specs,
        out_specs=P("narrow", "wide"),
        check_vma=False,
    )
```

```python
import functools
import math

import jax
import jax.numpy as jnp
from jax import lax
from jax.experimental import pallas as pl
from jax.experimental.pallas import tpu as pltpu
from jax.sharding import PartitionSpec as P

MESH = pl.DeviceIdType.MESH
TILE = 128
PIECES = (5, 4, 3, 2, 1)
GROUP_SLICES = 16
GROUP_TILES = 15
ROWS = 5


def kernel(
    cols_hbm,
    coeff_hbm,
    diag_hbm,
    vals_hbm,
    out_ref,
    cols_ref,
    coeff_v,
    diag_v,
    vals_v,
    x_ref,
    y_ref,
    yt_ref,
    acc_ref,
    alpha_ref,
    send_ref,
    back_ref,
    local_sem,
    pair_send,
    pair_recv,
    fwd_send,
    fwd_recv,
    ret_send,
    ret_recv,
    *,
    wide,
    scale,
):
    w = lax.axis_index("wide")
    n = lax.axis_index("narrow")
    other = 1 - n
    half = out_ref.shape[1] // TILE
    width = out_ref.shape[0]
    degree = cols_ref.shape[0]
    half_wide = wide // 2

    coeff_copy = pltpu.make_async_copy(coeff_hbm, coeff_v, local_sem.at[0])
    coeff_copy.start()
    vals_copy = pltpu.make_async_copy(vals_hbm, vals_v, local_sem.at[1])
    vals_copy.start()
    diag_copy = pltpu.make_async_copy(diag_hbm, diag_v, local_sem.at[2])
    diag_copy.start()
    cols_copy = pltpu.make_async_copy(cols_hbm, cols_ref, local_sem.at[3])
    cols_copy.start()

    barrier = pltpu.get_barrier_semaphore()

    def greet(step, carry):
        to = lax.rem(w + step, wide)

        @pl.when(step > 0)
        def _():
            pl.semaphore_signal(barrier, inc=1, device_id=(to, n), device_id_type=MESH)

        pl.semaphore_signal(barrier, inc=1, device_id=(to, other), device_id_type=MESH)
        return carry

    lax.fori_loop(0, wide, greet, 0, unroll=8)
    coeff_copy.wait()

    for i in range(half):
        x_ref[n * half + i] = coeff_v[:, i * TILE : (i + 1) * TILE].astype(jnp.bfloat16)

    pl.semaphore_wait(barrier, 2 * wide - 1)

    my_plane = lax.rem(w // 2, 2)
    side = lax.rem(my_plane + n, 2)
    quarter = half // 2
    starts = [sum(PIECES[:j]) for j in range(len(PIECES))]
    pair = []
    for j, piece in enumerate(PIECES + (quarter,)):
        if j < len(PIECES):
            part = x_ref.at[pl.ds(n * half + (1 - side) * quarter + starts[j], piece)]
        else:
            part = x_ref.at[pl.ds(n * half + side * quarter, quarter)]
        copy = pltpu.make_async_remote_copy(
            src_ref=part,
            dst_ref=part,
            send_sem=pair_send.at[j],
            recv_sem=pair_recv.at[j],
            device_id=(w, other),
            device_id_type=MESH,
        )
        if j < len(PIECES):
            copy.start()
        pair.append(copy)

    my_place = w // 4
    tile_half = lax.rem(w + my_plane + my_place, 2)
    active = my_place < quarter
    slot = side * quarter + my_place

    def send_forward(from_half, place):
        tile = from_half * half + side * quarter + place
        mine = jnp.logical_and(place == my_place, from_half == tile_half)

        @pl.when(mine)
        def _():
            pltpu.make_async_copy(x_ref.at[tile], y_ref.at[w], fwd_recv).start()

        @pl.when(jnp.logical_not(mine))
        def _():
            pltpu.make_async_remote_copy(
                src_ref=x_ref.at[tile],
                dst_ref=y_ref.at[w],
                send_sem=fwd_send,
                recv_sem=fwd_recv,
                device_id=(place * 4 + my_plane * 2 + lax.rem(from_half + my_plane + place, 2), n),
                device_id_type=MESH,
            ).start()

        pltpu.make_async_remote_copy(
            src_ref=x_ref.at[tile],
            dst_ref=y_ref.at[w],
            send_sem=fwd_send,
            recv_sem=fwd_recv,
            device_id=(
                place * 4 + (1 - my_plane) * 2 + lax.rem(from_half + 1 - my_plane + place, 2),
                other,
            ),
            device_id_type=MESH,
        ).start()

    def send_own(step, carry):
        send_forward(n, lax.rem(w * 7 + step, quarter))
        return carry

    lax.fori_loop(0, quarter, send_own, 0)

    for j, piece in enumerate(PIECES):
        pair[j].wait_recv()

        def send_relayed(step, carry):
            send_forward(other, starts[j] + lax.rem(w + step, piece))
            return carry

        lax.fori_loop(0, piece, send_relayed, 0)

    pair[-1].start()

    vals_copy.wait()
    cols_copy.wait()

    @pl.when(active)
    def _():
        pltpu.make_async_copy(y_ref, y_ref, fwd_recv).wait()

        def repack(g, carry):
            for t in range(GROUP_TILES):
                low, high = t * TILE, (t + 1) * TILE
                pieces = []
                while low < high:
                    source, begin = low // width, low % width
                    end = min(width, begin + high - low)
                    piece = y_ref[g * GROUP_SLICES + source].astype(jnp.float32)
                    pieces.append(piece[begin:end])
                    low += end - begin
                yt_ref[g * GROUP_TILES + t] = jnp.concatenate(pieces, axis=0).astype(
                    jnp.bfloat16
                )
            return carry

        lax.fori_loop(0, wide // GROUP_SLICES, repack, 0)

        def send_chunk(j):
            send_ref[j] = acc_ref[pl.ds(pl.multiple_of(j * width, 8), width), :].astype(
                jnp.bfloat16
            )
            to = n * half_wide + j
            mine = jnp.logical_and(to == w, tile_half == n)

            @pl.when(mine)
            def _():
                pltpu.make_async_copy(send_ref.at[j], back_ref.at[slot], ret_recv).start()

            @pl.when(jnp.logical_not(mine))
            def _():
                pltpu.make_async_remote_copy(
                    src_ref=send_ref.at[j],
                    dst_ref=back_ref.at[slot],
                    send_sem=ret_send,
                    recv_sem=ret_recv,
                    device_id=(to, tile_half),
                    device_id_type=MESH,
                ).start()

        groups = half // ROWS
        per_block = GROUP_TILES // ROWS
        first = lax.rem(w + w // 16, groups)

        def beta_group(step, carry):
            group = lax.rem(first + step, groups)
            for u in range(ROWS):
                row = group * ROWS + u
                lhs = jnp.concatenate([vals_v[row, k] for k in range(degree)], axis=1)
                rhs = jnp.concatenate([yt_ref[cols_ref[k, row]] for k in range(degree)], axis=0)
                acc_ref[pl.ds(pl.multiple_of(row * TILE, TILE), TILE), :] = jnp.dot(
                    lhs, rhs, preferred_element_type=jnp.float32
                )
            chunk = group * ROWS + group // per_block
            spot = lax.rem(group, per_block)

            @pl.when(jnp.logical_or(step > 0, spot == 0))
            def _():
                send_chunk(chunk)

            def send_rest(u, carry):
                send_chunk(chunk + u)
                return carry

            lax.fori_loop(1, jnp.where(spot == per_block - 1, ROWS + 1, ROWS), send_rest, 0)
            return carry

        lax.fori_loop(0, groups, beta_group, 0)

        @pl.when(lax.rem(first, per_block) != 0)
        def _():
            send_chunk(first * ROWS + first // per_block)

    pair[-1].wait_recv()

    def alpha_group(group, carry):
        for u in range(ROWS):
            row = group * ROWS + u
            lhs = jnp.concatenate([x_ref[cols_ref[k, row]] for k in range(degree)], axis=1)
            rhs = jnp.concatenate([vals_v[row, k] for k in range(degree)], axis=1)
            alpha_ref[row] = lax.dot_general(
                lhs, rhs, (((1,), (1,)), ((), ())), preferred_element_type=jnp.float32
            )
        return carry

    lax.fori_loop(0, half // ROWS, alpha_group, 0)

    diag_copy.wait()
    for i in range(half):
        part = slice(i * TILE, (i + 1) * TILE)
        out_ref[:, part] = scale * alpha_ref[i] + diag_v[:, part] * coeff_v[:, part]

    pltpu.make_async_copy(back_ref, back_ref, ret_recv).wait()
    for i in range(half):
        part = slice(i * TILE, (i + 1) * TILE)
        out_ref[:, part] += scale * back_ref[i].astype(jnp.float32)

    for copy in pair:
        copy.wait_send()

    @pl.when(active)
    def _():
        done = x_ref.at[pl.ds(0, 2 * half - 1)]
        pltpu.make_async_copy(done, done, fwd_send).wait()

    @pl.when(jnp.logical_not(active))
    def _():
        pltpu.make_async_copy(x_ref, x_ref, fwd_send).wait()

    own_return = jnp.logical_and(tile_half == n, w // half_wide == n)

    @pl.when(jnp.logical_and(active, own_return))
    def _():
        done = send_ref.at[pl.ds(0, half_wide - 1)]
        pltpu.make_async_copy(done, done, ret_send).wait()

    @pl.when(jnp.logical_and(active, jnp.logical_not(own_return)))
    def _():
        pltpu.make_async_copy(send_ref, send_ref, ret_send).wait()


def solution(mesh):
    wide = mesh.shape["wide"]

    def per_device(coeffs, diagonal, tile_cols, tile_vals):
        rows, width = coeffs.shape
        half, degree = tile_cols.shape
        scale = 1.0 / math.sqrt(degree * TILE)
        any_space = pl.BlockSpec(memory_space=pl.ANY)
        out = pl.pallas_call(
            functools.partial(kernel, wide=wide, scale=scale),
            out_shape=jax.ShapeDtypeStruct((width, rows), jnp.float32),
            in_specs=[
                any_space,
                any_space,
                any_space,
                any_space,
            ],
            out_specs=pl.BlockSpec(memory_space=pltpu.VMEM),
            scratch_shapes=[
                pltpu.SMEM((degree, half), jnp.int32),
                pltpu.VMEM((width, rows), jnp.float32),
                pltpu.VMEM((width, rows), jnp.float32),
                pltpu.VMEM((half, degree, TILE, TILE), jnp.bfloat16),
                pltpu.VMEM((2 * half, width, TILE), jnp.bfloat16),
                pltpu.VMEM((wide, width, TILE), jnp.bfloat16),
                pltpu.VMEM((2 * half, TILE, TILE), jnp.bfloat16),
                pltpu.VMEM((rows, TILE), jnp.float32),
                pltpu.VMEM((half, width, TILE), jnp.float32),
                pltpu.VMEM((wide // 2, width, TILE), jnp.bfloat16),
                pltpu.VMEM((half, width, TILE), jnp.bfloat16),
                pltpu.SemaphoreType.DMA((4,)),
                pltpu.SemaphoreType.DMA((len(PIECES) + 1,)),
                pltpu.SemaphoreType.DMA((len(PIECES) + 1,)),
                pltpu.SemaphoreType.DMA,
                pltpu.SemaphoreType.DMA,
                pltpu.SemaphoreType.DMA,
                pltpu.SemaphoreType.DMA,
            ],
            compiler_params=pltpu.CompilerParams(
                collective_id=0, has_side_effects=True, vmem_limit_bytes=52 * 1024 * 1024
            ),
        )(tile_cols.T, coeffs.T, diagonal.T, tile_vals)
        return out.T

    in_specs = (
        P("narrow", "wide"),
        P("narrow", "wide"),
        P("narrow", None),
        P("narrow", None, None, None),
    )
    return jax.shard_map(
        per_device,
        mesh=mesh,
        in_specs=in_specs,
        out_specs=P("narrow", "wide"),
        check_vma=False,
    )
```

```python
import functools
import math

import jax
import jax.numpy as jnp
from jax import lax
from jax.experimental import pallas as pl
from jax.experimental.pallas import tpu as pltpu
from jax.sharding import PartitionSpec as P

MESH = pl.DeviceIdType.MESH
TILE = 128
PIECES = (5, 4, 3, 2, 1)
GROUP_SLICES = 16
GROUP_TILES = 15
ROWS = 5


def kernel(
    cols_hbm,
    coeff_hbm,
    diag_hbm,
    vals_hbm,
    out_ref,
    cols_ref,
    coeff_v,
    diag_v,
    vals_v,
    x_ref,
    y_ref,
    yt_ref,
    acc_ref,
    alpha_ref,
    send_ref,
    back_ref,
    local_sem,
    pair_send,
    pair_recv,
    fwd_send,
    fwd_recv,
    ret_send,
    ret_recv,
    *,
    wide,
    scale,
):
    w = lax.axis_index("wide")
    n = lax.axis_index("narrow")
    other = 1 - n
    half = out_ref.shape[1] // TILE
    width = out_ref.shape[0]
    degree = cols_ref.shape[0]
    half_wide = wide // 2

    coeff_copy = pltpu.make_async_copy(coeff_hbm, coeff_v, local_sem.at[0])
    coeff_copy.start()
    vals_copy = pltpu.make_async_copy(vals_hbm, vals_v, local_sem.at[1])
    vals_copy.start()
    diag_copy = pltpu.make_async_copy(diag_hbm, diag_v, local_sem.at[2])
    diag_copy.start()
    cols_copy = pltpu.make_async_copy(cols_hbm, cols_ref, local_sem.at[3])
    cols_copy.start()

    barrier = pltpu.get_barrier_semaphore()

    def greet(step, carry):
        to = lax.rem(w + step, wide)

        @pl.when(step > 0)
        def _():
            pl.semaphore_signal(barrier, inc=1, device_id=(to, n), device_id_type=MESH)

        pl.semaphore_signal(barrier, inc=1, device_id=(to, other), device_id_type=MESH)
        return carry

    lax.fori_loop(0, wide, greet, 0, unroll=32)
    coeff_copy.wait()

    for i in range(half):
        x_ref[n * half + i] = coeff_v[:, i * TILE : (i + 1) * TILE].astype(jnp.bfloat16)

    pl.semaphore_wait(barrier, 2 * wide - 1)

    my_plane = lax.rem(w // 2, 2)
    side = lax.rem(my_plane + n, 2)
    quarter = half // 2
    starts = [sum(PIECES[:j]) for j in range(len(PIECES))]
    pair = []
    for j, piece in enumerate(PIECES + (quarter,)):
        if j < len(PIECES):
            part = x_ref.at[pl.ds(n * half + (1 - side) * quarter + starts[j], piece)]
        else:
            part = x_ref.at[pl.ds(n * half + side * quarter, quarter)]
        copy = pltpu.make_async_remote_copy(
            src_ref=part,
            dst_ref=part,
            send_sem=pair_send.at[j],
            recv_sem=pair_recv.at[j],
            device_id=(w, other),
            device_id_type=MESH,
        )
        if j < len(PIECES):
            copy.start()
        pair.append(copy)

    my_place = w // 4
    tile_half = lax.rem(w + my_plane + my_place, 2)
    active = my_place < quarter
    slot = side * quarter + my_place

    def send_forward(from_half, place):
        tile = from_half * half + side * quarter + place
        mine = jnp.logical_and(place == my_place, from_half == tile_half)

        @pl.when(mine)
        def _():
            pltpu.make_async_copy(x_ref.at[tile], y_ref.at[w], fwd_recv).start()

        @pl.when(jnp.logical_not(mine))
        def _():
            pltpu.make_async_remote_copy(
                src_ref=x_ref.at[tile],
                dst_ref=y_ref.at[w],
                send_sem=fwd_send,
                recv_sem=fwd_recv,
                device_id=(place * 4 + my_plane * 2 + lax.rem(from_half + my_plane + place, 2), n),
                device_id_type=MESH,
            ).start()

        pltpu.make_async_remote_copy(
            src_ref=x_ref.at[tile],
            dst_ref=y_ref.at[w],
            send_sem=fwd_send,
            recv_sem=fwd_recv,
            device_id=(
                place * 4 + (1 - my_plane) * 2 + lax.rem(from_half + 1 - my_plane + place, 2),
                other,
            ),
            device_id_type=MESH,
        ).start()

    def send_own(step, carry):
        send_forward(n, lax.rem(w * 7 + step, quarter))
        return carry

    lax.fori_loop(0, quarter, send_own, 0)

    for j, piece in enumerate(PIECES):
        pair[j].wait_recv()

        def send_relayed(step, carry):
            send_forward(other, starts[j] + lax.rem(w + step, piece))
            return carry

        lax.fori_loop(0, piece, send_relayed, 0)

    pair[-1].start()

    vals_copy.wait()
    cols_copy.wait()

    @pl.when(active)
    def _():
        pltpu.make_async_copy(y_ref, y_ref, fwd_recv).wait()

        def repack(g, carry):
            for t in range(GROUP_TILES):
                low, high = t * TILE, (t + 1) * TILE
                pieces = []
                while low < high:
                    source, begin = low // width, low % width
                    end = min(width, begin + high - low)
                    piece = y_ref[g * GROUP_SLICES + source].astype(jnp.float32)
                    pieces.append(piece[begin:end])
                    low += end - begin
                yt_ref[g * GROUP_TILES + t] = jnp.concatenate(pieces, axis=0).astype(
                    jnp.bfloat16
                )
            return carry

        lax.fori_loop(0, wide // GROUP_SLICES, repack, 0)

        def send_chunk(j):
            send_ref[j] = acc_ref[pl.ds(pl.multiple_of(j * width, 8), width), :].astype(
                jnp.bfloat16
            )
            to = n * half_wide + j
            mine = jnp.logical_and(to == w, tile_half == n)

            @pl.when(mine)
            def _():
                pltpu.make_async_copy(send_ref.at[j], back_ref.at[slot], ret_recv).start()

            @pl.when(jnp.logical_not(mine))
            def _():
                pltpu.make_async_remote_copy(
                    src_ref=send_ref.at[j],
                    dst_ref=back_ref.at[slot],
                    send_sem=ret_send,
                    recv_sem=ret_recv,
                    device_id=(to, tile_half),
                    device_id_type=MESH,
                ).start()

        groups = half // ROWS
        per_block = GROUP_TILES // ROWS
        first = lax.rem(w + w // 16, groups)

        def beta_group(step, carry):
            group = lax.rem(first + step, groups)
            for u in range(ROWS):
                row = group * ROWS + u
                lhs = jnp.concatenate([vals_v[row, k] for k in range(degree)], axis=1)
                rhs = jnp.concatenate([yt_ref[cols_ref[k, row]] for k in range(degree)], axis=0)
                acc_ref[pl.ds(pl.multiple_of(row * TILE, TILE), TILE), :] = jnp.dot(
                    lhs, rhs, preferred_element_type=jnp.float32
                )
            chunk = group * ROWS + group // per_block
            spot = lax.rem(group, per_block)

            @pl.when(jnp.logical_or(step > 0, spot == 0))
            def _():
                send_chunk(chunk)

            def send_rest(u, carry):
                send_chunk(chunk + u)
                return carry

            lax.fori_loop(1, jnp.where(spot == per_block - 1, ROWS + 1, ROWS), send_rest, 0)
            return carry

        lax.fori_loop(0, groups, beta_group, 0)

        @pl.when(lax.rem(first, per_block) != 0)
        def _():
            send_chunk(first * ROWS + first // per_block)

    pair[-1].wait_recv()

    def alpha_group(group, carry):
        for u in range(ROWS):
            row = group * ROWS + u
            lhs = jnp.concatenate([x_ref[cols_ref[k, row]] for k in range(degree)], axis=1)
            rhs = jnp.concatenate([vals_v[row, k] for k in range(degree)], axis=1)
            alpha_ref[row] = lax.dot_general(
                lhs, rhs, (((1,), (1,)), ((), ())), preferred_element_type=jnp.float32
            )
        return carry

    lax.fori_loop(0, half // ROWS, alpha_group, 0)

    diag_copy.wait()
    for i in range(half):
        part = slice(i * TILE, (i + 1) * TILE)
        out_ref[:, part] = scale * alpha_ref[i] + diag_v[:, part] * coeff_v[:, part]

    pltpu.make_async_copy(back_ref, back_ref, ret_recv).wait()
    for i in range(half):
        part = slice(i * TILE, (i + 1) * TILE)
        out_ref[:, part] += scale * back_ref[i].astype(jnp.float32)

    for copy in pair:
        copy.wait_send()

    @pl.when(active)
    def _():
        done = x_ref.at[pl.ds(0, 2 * half - 1)]
        pltpu.make_async_copy(done, done, fwd_send).wait()

    @pl.when(jnp.logical_not(active))
    def _():
        pltpu.make_async_copy(x_ref, x_ref, fwd_send).wait()

    own_return = jnp.logical_and(tile_half == n, w // half_wide == n)

    @pl.when(jnp.logical_and(active, own_return))
    def _():
        done = send_ref.at[pl.ds(0, half_wide - 1)]
        pltpu.make_async_copy(done, done, ret_send).wait()

    @pl.when(jnp.logical_and(active, jnp.logical_not(own_return)))
    def _():
        pltpu.make_async_copy(send_ref, send_ref, ret_send).wait()


def solution(mesh):
    wide = mesh.shape["wide"]

    def per_device(coeffs, diagonal, tile_cols, tile_vals):
        rows, width = coeffs.shape
        half, degree = tile_cols.shape
        scale = 1.0 / math.sqrt(degree * TILE)
        any_space = pl.BlockSpec(memory_space=pl.ANY)
        out = pl.pallas_call(
            functools.partial(kernel, wide=wide, scale=scale),
            out_shape=jax.ShapeDtypeStruct((width, rows), jnp.float32),
            in_specs=[
                any_space,
                any_space,
                any_space,
                any_space,
            ],
            out_specs=pl.BlockSpec(memory_space=pltpu.VMEM),
            scratch_shapes=[
                pltpu.SMEM((degree, half), jnp.int32),
                pltpu.VMEM((width, rows), jnp.float32),
                pltpu.VMEM((width, rows), jnp.float32),
                pltpu.VMEM((half, degree, TILE, TILE), jnp.bfloat16),
                pltpu.VMEM((2 * half, width, TILE), jnp.bfloat16),
                pltpu.VMEM((wide, width, TILE), jnp.bfloat16),
                pltpu.VMEM((2 * half, TILE, TILE), jnp.bfloat16),
                pltpu.VMEM((rows, TILE), jnp.float32),
                pltpu.VMEM((half, width, TILE), jnp.float32),
                pltpu.VMEM((wide // 2, width, TILE), jnp.bfloat16),
                pltpu.VMEM((half, width, TILE), jnp.bfloat16),
                pltpu.SemaphoreType.DMA((4,)),
                pltpu.SemaphoreType.DMA((len(PIECES) + 1,)),
                pltpu.SemaphoreType.DMA((len(PIECES) + 1,)),
                pltpu.SemaphoreType.DMA,
                pltpu.SemaphoreType.DMA,
                pltpu.SemaphoreType.DMA,
                pltpu.SemaphoreType.DMA,
            ],
            compiler_params=pltpu.CompilerParams(
                collective_id=0, has_side_effects=True, vmem_limit_bytes=52 * 1024 * 1024
            ),
        )(tile_cols.T, coeffs.T, diagonal.T, tile_vals)
        return out.T

    in_specs = (
        P("narrow", "wide"),
        P("narrow", "wide"),
        P("narrow", None),
        P("narrow", None, None, None),
    )
    return jax.shard_map(
        per_device,
        mesh=mesh,
        in_specs=in_specs,
        out_specs=P("narrow", "wide"),
        check_vma=False,
    )
```
